32 devices in a mesh: pair: 8 (over z, y), seg: 4 (over x, core).
Axes of the slice: x: 2, y: 2, z: 4, core: 2. Of those that a mesh axis runs over, the one named last changes fastest.
Arguments:
- traces: bfloat16 [8, 128, 32768], P('pair', None, 'seg'), may hold values from -6 to 6
- pairs: int32 [8, 2], P('pair'), may hold values from 0 to 7
- block_row: int32 [8], replicated, may hold values from 0 to 7, each once
Outputs:
- stack: float32 [8, 128, 2048], P('pair', 'seg')
The draws below stay inside these ranges and needn't reach their ends.
Inputs may be any that keep to these rules, and one draw needn't show every extreme that they name: `pairs`: each entry is a block number. `block_row`: a permutation of the block numbers.
All inputs are finite; a program needn't handle non-finite values.
Results may differ from the reference program's by a relative error of at most 0.0044.
Values may be sent and summed in bfloat16 or wider, within the bound.
No kernel may reach another device: no remote copies, remote signals or barrier semaphores. Data moves between devices by JAX's collectives and lax.ppermute only.
A program may use at most 64 MiB of HBM per device.

```python
import math
import jax
import jax.numpy as jnp
import numpy as np
from jax import lax

CH = 128
WIN = 2048
NB = 512
LAGS = 2048
WIN_DEV = 4
BLOCKS = 8
PAIRS = 8
SAMPLES = 32768
N_SEG = 4


def place_ends(values, own_key, smallest, top_value):
    shape = values.shape
    index_at = [jax.random.randint(jax.random.fold_in(own_key, axis), (), 0, shape[axis]) for axis in range(len(shape))]
    values = values.at[tuple(index_at)].set(smallest)
    longest = shape.index(max(shape))
    index_at[longest] = (index_at[longest] + 1) % shape[longest]
    return values.at[tuple(index_at)].set(top_value)


def block_scale(rng, extent, split, least, largest):
    level = 1.0
    for axis_at, blocks in split:
        draws = jax.random.uniform(jax.random.fold_in(jax.random.fold_in(rng, 6), axis_at), (blocks,), jnp.float32, least / len(split), largest / len(split))
        level = level * jnp.repeat(jnp.exp(draws), extent[axis_at] // blocks).reshape((-1,) + (1,) * (len(extent) - 1 - axis_at))
    return level


def cumulative_ranks(count, skew):
    weights = [(1 << 20) // math.isqrt(grade ** skew) + 1 for grade in range(1, count + 1)]
    scale = 1 + sum(weights) // (1 << 30)
    return np.cumsum(np.array([max(1, weight // scale) for weight in weights]))


def ranked_ids(key, extent, count, skew):
    listing = cumulative_ranks(count, skew)
    pick = jax.random.randint(jax.random.fold_in(key, 1), extent, 0, int(listing[count - 1]))
    rank = jnp.searchsorted(jnp.asarray(listing, jnp.int32), pick, side="right")
    return jax.random.permutation(jax.random.fold_in(key, 2), count)[rank].astype(jnp.int32)


def noise(key, extent, scale, reach, split=(), kind=jnp.bfloat16):
    level = block_scale(key, extent, split, -0.22, 0.18) if split else 1.0
    entries = jax.random.normal(key, extent, jnp.float32) * scale * level
    return jnp.minimum(jnp.maximum(entries, -reach), reach).astype(kind)


def setup_inputs(seed: int = 0) -> dict:
    key_list = jax.random.split(jax.random.key(seed), 4)
    traces = noise(key_list[0], (BLOCKS, CH, SAMPLES), 1.0, 6.0, ((0, 8), (2, 4)))
    pairs = place_ends(ranked_ids(key_list[1], (PAIRS, 2), BLOCKS, 2), jax.random.fold_in(key_list[1], 3), 0, BLOCKS - 1).astype(jnp.int32)
    block_row = jax.random.permutation(key_list[2], BLOCKS).astype(jnp.int32)
    return {"traces": traces, "pairs": pairs, "block_row": block_row}


def forward_table(bins, width):
    freq = jnp.arange(bins, dtype=jnp.int32) + 1
    times = jnp.arange(width, dtype=jnp.int32)
    phase = (freq[:, None] * times[None, :] % width).astype(jnp.float32) * (2.0 * jnp.pi / width)
    return jnp.stack((jnp.cos(phase), -jnp.sin(phase))).astype(jnp.bfloat16)

def inverse_table(bins, lags, width):
    freq = jnp.arange(bins, dtype=jnp.int32) + 1
    shifts = jnp.arange(lags, dtype=jnp.int32) - lags // 2
    phase = (freq[:, None] * shifts[None, :] % width).astype(jnp.float32) * (2.0 * jnp.pi / width)
    return jnp.stack((jnp.cos(phase), -jnp.sin(phase)))

def reference(traces, pairs, block_row):
    frames = WIN_DEV * N_SEG
    table = forward_table(NB, WIN).astype(jnp.float32)

    def whiten(block):
        windows = block.reshape(CH, frames, WIN).astype(jnp.float32)
        spectra = jnp.einsum('skt,cwt->skwc', table, windows)
        power = lax.optimization_barrier(jnp.mean(spectra[0] * spectra[0] + spectra[1] * spectra[1], axis=-1))
        return (spectra / jnp.sqrt(power + 1e-06)[None, :, :, None]).astype(jnp.bfloat16)
    whitened = lax.map(whiten, traces)
    rows_first = block_row[pairs[:, 0]].astype(jnp.int32)
    rows_second = block_row[pairs[:, 1]].astype(jnp.int32)
    back = inverse_table(NB, LAGS, WIN)

    def correlate(rows):
        first = whitened[rows[0]].astype(jnp.float32)
        second = whitened[rows[1]].astype(jnp.float32)
        real = lax.optimization_barrier(jnp.sum(first[0] * second[0] + first[1] * second[1], axis=1))
        imag = lax.optimization_barrier(jnp.sum(first[0] * second[1] - first[1] * second[0], axis=1))
        cross = jnp.stack((real, imag))
        return jnp.einsum('skc,skl->cl', cross, back, precision=lax.Precision.HIGHEST) / frames
    return lax.map(correlate, jnp.stack((rows_first, rows_second), axis=1))
```

```python
import functools

import jax
import jax.numpy as jnp
import ml_dtypes
import numpy as np
from jax import lax
from jax.experimental import pallas as pl
from jax.experimental.pallas import tpu as pltpu
from jax.sharding import PartitionSpec as P

WIN = 2048
NB = 512
LAGS = 2048
HALF = WIN // 2
LANES = 128
BINS = LANES // 2
TILES = NB // BINS
GROUP = 2


def frequencies():
    even = np.arange(2, NB + 1, 2)
    odd = np.arange(1, NB + 1, 2)
    return np.concatenate((even, odd)).reshape(TILES, BINS)


def forward_table():
    phase = (frequencies()[:, :, None] * np.arange(HALF) % WIN) * (2.0 * np.pi / WIN)
    table = np.stack((np.cos(phase), -np.sin(phase)), axis=1)
    return table.reshape(TILES * LANES, HALF).T.astype(ml_dtypes.bfloat16)


def inverse_table(scale):
    shifts = np.arange(LAGS // 2) - LAGS // 2
    phase = (frequencies()[:, :, None] * shifts % WIN) * (2.0 * np.pi / WIN)
    table = np.stack((np.cos(phase), -np.sin(phase)), axis=1) * scale
    return table.reshape(TILES * LANES, LAGS // 2).astype(ml_dtypes.bfloat16)


def whiten_kernel(windows, segs, traces_ref, table_ref, out_ref):
    channels = traces_ref.shape[0]
    halves = [traces_ref[:, k * HALF : (k + 1) * HALF] for k in range(2 * windows)]
    product = jnp.dot(
        jnp.concatenate(halves, axis=0), table_ref[...], preferred_element_type=jnp.float32
    )
    sign = jnp.where(pl.program_id(0) * GROUP < TILES // 2, 1.0, -1.0)
    for w in range(windows):
        first = product[2 * w * channels : (2 * w + 1) * channels]
        second = product[(2 * w + 1) * channels : (2 * w + 2) * channels]
        spectra = first + sign * second
        power = jnp.sum(spectra * spectra, axis=0, keepdims=True) * (1.0 / channels)
        for tile in range(GROUP):
            cols = slice(tile * LANES, (tile + 1) * LANES)
            both = power[:, cols]
            both = both + pltpu.roll(both, BINS, 1)
            white = spectra[:, cols] * lax.rsqrt(both + 1e-06)
            out_ref[tile, :, w] = white.astype(jnp.bfloat16).reshape(segs, channels // segs, LANES)


def whiten(traces, windows, segs):
    channels, samples = traces.shape
    shape = (TILES, segs, windows, channels // segs, LANES)
    return pl.pallas_call(
        functools.partial(whiten_kernel, windows, segs),
        grid=(TILES // GROUP,),
        in_specs=[
            pl.BlockSpec((channels, samples), lambda i: (0, 0)),
            pl.BlockSpec((HALF, GROUP * LANES), lambda i: (0, i)),
        ],
        out_specs=pl.BlockSpec((GROUP,) + shape[1:], lambda i: (i, 0, 0, 0, 0)),
        out_shape=jax.ShapeDtypeStruct(shape, jnp.bfloat16),
        compiler_params=pltpu.CompilerParams(vmem_limit_bytes=24 * 2**20),
        name="whiten",
    )(traces, jnp.asarray(forward_table()))


def cross_kernel(pairs_ref, row_ref, spectra_ref, out_ref):
    count, channels, lanes = out_ref.shape
    frames = spectra_ref.shape[1]
    low = lax.broadcasted_iota(jnp.int32, (channels, lanes), 1) < lanes // 2

    def one(i, carry):
        a = row_ref[pairs_ref[i, 0]]
        b = row_ref[pairs_ref[i, 1]]
        straight = jnp.zeros((channels, lanes), jnp.float32)
        crossed = jnp.zeros((channels, lanes), jnp.float32)
        for w in range(frames):
            first = spectra_ref[a, w].astype(jnp.float32)
            second = spectra_ref[b, w].astype(jnp.float32)
            straight += first * second
            crossed += first * pltpu.roll(second, lanes // 2, 1)
        real = straight + pltpu.roll(straight, lanes // 2, 1)
        imag = pltpu.roll(crossed, lanes // 2, 1) - crossed
        out_ref[i] = jnp.where(low, real, imag).astype(jnp.bfloat16)
        return carry

    lax.fori_loop(0, count, one, 0)


def cross_tiles(pairs, block_row, spectra):
    rows, frames, channels, lanes = spectra.shape
    smem = pl.BlockSpec(memory_space=pltpu.SMEM)
    vmem = pl.BlockSpec(memory_space=pltpu.VMEM)
    return pl.pallas_call(
        cross_kernel,
        in_specs=[smem, smem, vmem],
        out_specs=vmem,
        out_shape=jax.ShapeDtypeStruct((pairs.shape[0], channels, lanes), jnp.bfloat16),
        compiler_params=pltpu.CompilerParams(vmem_limit_bytes=8 * 2**20),
        name="cross",
    )(pairs, block_row, spectra)


def cross_bands(pairs, block_row, spectra):
    rows, frames, channels, lanes = spectra.shape
    parts = spectra.reshape(rows, frames, channels, 2, lanes // 2)
    first = parts[block_row[pairs[:, 0]]].astype(jnp.float32)
    second = parts[block_row[pairs[:, 1]]].astype(jnp.float32)
    real = jnp.sum(first[:, :, :, 0] * second[:, :, :, 0] + first[:, :, :, 1] * second[:, :, :, 1], axis=1)
    imag = jnp.sum(first[:, :, :, 0] * second[:, :, :, 1] - first[:, :, :, 1] * second[:, :, :, 0], axis=1)
    return jnp.concatenate((real, imag), axis=2).astype(jnp.bfloat16)


def inverse_kernel(cross_ref, table_ref, out_ref):
    half = TILES // 2
    even = jnp.concatenate([cross_ref[k] for k in range(half)], axis=1)
    odd = jnp.concatenate([cross_ref[k] for k in range(half, TILES)], axis=1)
    depth = half * LANES
    a = jnp.dot(even, table_ref[:depth], preferred_element_type=jnp.float32)
    b = jnp.dot(odd, table_ref[depth:], preferred_element_type=jnp.float32)
    out_ref[0, :, : LAGS // 2] = a + b
    out_ref[0, :, LAGS // 2 :] = a - b


def inverse(cross, scale):
    vmem = pl.BlockSpec(memory_space=pltpu.VMEM)
    return pl.pallas_call(
        inverse_kernel,
        in_specs=[vmem, vmem],
        out_specs=vmem,
        out_shape=jax.ShapeDtypeStruct((1, cross.shape[1], LAGS), jnp.float32),
        compiler_params=pltpu.CompilerParams(vmem_limit_bytes=16 * 2**20),
        name="inverse",
    )(cross, jnp.asarray(inverse_table(scale)))


def local(traces, pairs, block_row):
    _, channels, samples = traces.shape
    windows = samples // WIN
    bands, segs = lax.axis_size("pair"), lax.axis_size("seg")
    per_tile = bands // TILES
    share = channels // segs
    width = 2 * NB // bands
    all_pairs = lax.all_gather(pairs, "pair", axis=0, tiled=True)
    white = whiten(traces[0], windows, segs)
    if per_tile > 1:
        white = white.reshape(TILES, segs, windows, share, 2, per_tile, width // 2)
        white = white.transpose(0, 5, 1, 2, 3, 4, 6)
    sent = white.reshape(bands * segs, windows, share, width)
    held = lax.all_to_all(sent, ("pair", "seg"), split_axis=0, concat_axis=0, tiled=True)
    held = held.reshape(bands, segs * windows, share, width)
    cross_of = cross_tiles if width == LANES else cross_bands
    cross = cross_of(all_pairs, block_row, held)
    mine = lax.all_to_all(cross, "pair", split_axis=0, concat_axis=0, tiled=True)
    if per_tile > 1:
        mine = mine.reshape(TILES, per_tile, share, 2, width // 2).transpose(0, 2, 3, 1, 4)
        mine = mine.reshape(TILES, share, LANES)
    return inverse(mine, 1.0 / (windows * segs))


def solution(mesh):
    placed = (P("pair", None, "seg"), P("pair", None), P())
    return jax.shard_map(
        local, mesh=mesh, in_specs=placed, out_specs=P("pair", "seg", None), check_vma=False
    )
```

```python
import functools

import jax
import jax.numpy as jnp
import ml_dtypes
import numpy as np
from jax import lax
from jax.experimental import pallas as pl
from jax.experimental.pallas import tpu as pltpu
from jax.sharding import PartitionSpec as P

WIN = 2048
NB = 512
LAGS = 2048
HALF = WIN // 2
BINS = 128
GROUPS = NB // BINS
SPLIT = 2
PARITIES = 2
NOTE = 8


def frequencies():
    even = np.arange(2, NB + 1, 2)
    odd = np.arange(1, NB + 1, 2)
    return np.concatenate((even, odd)).reshape(GROUPS, BINS)


def forward_table():
    phase = (frequencies()[:, :, None] * np.arange(HALF) % WIN) * (2.0 * np.pi / WIN)
    table = np.stack((np.cos(phase), -np.sin(phase)), axis=1).reshape(PARITIES, NB, HALF)
    return np.ascontiguousarray(table.transpose(0, 2, 1)).astype(ml_dtypes.bfloat16)


def inverse_table(scale):
    shifts = np.arange(LAGS // 2) - LAGS // 2
    phase = (frequencies()[:, :, None] * shifts % WIN) * (2.0 * np.pi / WIN)
    table = np.stack((np.cos(phase), -np.sin(phase)), axis=1) * scale
    return table.reshape(2 * NB, LAGS // 2).astype(ml_dtypes.bfloat16)


def whiten_kernel(windows, segs, pairs_ref, row_ref, traces_hbm, table_hbm, out_hbm, frames, table, sent, frame_sem, table_sem, sent_sem):
    channels = frames.shape[1]
    share = channels // segs // SPLIT
    loads = [
        pltpu.make_async_copy(traces_hbm.at[:, pl.ds(w * WIN, WIN)], frames.at[w], frame_sem.at[w])
        for w in range(windows)
    ]
    tables = [
        pltpu.make_async_copy(table_hbm.at[i], table.at[i], table_sem.at[i]) for i in range(PARITIES)
    ]
    per = GROUPS // PARITIES
    stores = [
        pltpu.make_async_copy(sent.at[pl.ds(i * per, per)], out_hbm.at[pl.ds(i * per, per)], sent_sem.at[i])
        for i in range(PARITIES)
    ]
    tables[0].start()
    for load in loads:
        load.start()
    tables[1].start()
    first_row = row_ref[pairs_ref[0, 0]].astype(jnp.float32)
    second_row = row_ref[pairs_ref[0, 1]].astype(jnp.float32)
    line = lax.broadcasted_iota(jnp.int32, (NOTE, BINS), 0)
    note = jnp.where(line == 0, first_row, second_row).astype(jnp.bfloat16)
    sent[:, :, :, 2 * windows * share :] = jnp.broadcast_to(note, (GROUPS, SPLIT, segs, NOTE, BINS))
    for load in loads:
        load.wait()
    for i in range(PARITIES):
        tables[i].wait()
        for w in range(windows):
            halves = jnp.concatenate((frames[w, :, :HALF], frames[w, :, HALF:]), axis=0)
            product = jnp.dot(halves, table[i], preferred_element_type=jnp.float32)
            first, second = product[:channels], product[channels:]
            spectra = first + second if i == 0 else first - second
            for k in range(per):
                real = spectra[:, 2 * k * BINS : (2 * k + 1) * BINS]
                imag = spectra[:, (2 * k + 1) * BINS : (2 * k + 2) * BINS]
                power = jnp.sum(real * real + imag * imag, axis=0, keepdims=True) * (1.0 / channels)
                gain = lax.rsqrt(power + 1e-06)
                for part, values in enumerate((real, imag)):
                    white = (values * gain).astype(jnp.bfloat16).reshape(segs, SPLIT, share, BINS)
                    at = (2 * w + part) * share
                    for h in range(SPLIT):
                        sent[i * per + k, h, :, at : at + share] = white[:, h]
        stores[i].start()
    for store in stores:
        store.wait()


def whiten(pairs, block_row, traces, windows, segs):
    channels = traces.shape[0]
    share = channels // segs // SPLIT
    shape = (GROUPS, SPLIT, segs, 2 * windows * share + NOTE, BINS)
    hbm = pl.BlockSpec(memory_space=pl.ANY)
    smem = pl.BlockSpec(memory_space=pltpu.SMEM)
    return pl.pallas_call(
        functools.partial(whiten_kernel, windows, segs),
        in_specs=[smem, smem, hbm, hbm],
        out_specs=hbm,
        out_shape=jax.ShapeDtypeStruct(shape, jnp.bfloat16),
        scratch_shapes=[
            pltpu.VMEM((windows, channels, WIN), jnp.bfloat16),
            pltpu.VMEM((PARITIES, HALF, NB), jnp.bfloat16),
            pltpu.VMEM(shape, jnp.bfloat16),
            pltpu.SemaphoreType.DMA((windows,)),
            pltpu.SemaphoreType.DMA((PARITIES,)),
            pltpu.SemaphoreType.DMA((PARITIES,)),
        ],
        compiler_params=pltpu.CompilerParams(vmem_limit_bytes=56 * 2**20),
        name="whiten",
    )(pairs, block_row, traces, jnp.asarray(forward_table()))


def cross_kernel(windows, spectra_ref, out_ref):
    segs = spectra_ref.shape[1]
    share = out_ref.shape[2]
    notes = [spectra_ref[i, 0, 2 * windows * share :].astype(jnp.float32) for i in range(out_ref.shape[0])]
    rows = [(note[0, 0].astype(jnp.int32), note[1, 0].astype(jnp.int32)) for note in notes]
    for i, (a, b) in enumerate(rows):
        real = jnp.zeros(out_ref.shape[2:], jnp.float32)
        imag = jnp.zeros(out_ref.shape[2:], jnp.float32)
        for s in range(segs):
            for w in range(windows):
                re = slice(2 * w * share, (2 * w + 1) * share)
                im = slice((2 * w + 1) * share, (2 * w + 2) * share)
                first_re = spectra_ref[a, s, re].astype(jnp.float32)
                first_im = spectra_ref[a, s, im].astype(jnp.float32)
                second_re = spectra_ref[b, s, re].astype(jnp.float32)
                second_im = spectra_ref[b, s, im].astype(jnp.float32)
                real += first_re * second_re + first_im * second_im
                imag += first_re * second_im - first_im * second_re
        out_ref[i, 0] = real.astype(jnp.bfloat16)
        out_ref[i, 1] = imag.astype(jnp.bfloat16)


def cross_groups(spectra, windows, share):
    vmem = pl.BlockSpec(memory_space=pltpu.VMEM)
    return pl.pallas_call(
        functools.partial(cross_kernel, windows),
        in_specs=[vmem],
        out_specs=vmem,
        out_shape=jax.ShapeDtypeStruct((spectra.shape[0], 2, share, BINS), jnp.bfloat16),
        compiler_params=pltpu.CompilerParams(vmem_limit_bytes=8 * 2**20),
        name="cross",
    )(spectra)


def cross_narrow(spectra, windows, share):
    parts, segs, rows, width = spectra.shape
    noted = spectra[:, 0, rows - NOTE : rows - NOTE + 2, 0].astype(jnp.int32)
    parted = spectra[:, :, : rows - NOTE].reshape(parts, segs * windows, 2, share, width)
    first = parted[noted[:, 0]].astype(jnp.float32)
    second = parted[noted[:, 1]].astype(jnp.float32)
    real = jnp.sum(first[:, :, 0] * second[:, :, 0] + first[:, :, 1] * second[:, :, 1], axis=1)
    imag = jnp.sum(first[:, :, 0] * second[:, :, 1] - first[:, :, 1] * second[:, :, 0], axis=1)
    return jnp.stack((real, imag), axis=1).astype(jnp.bfloat16)


def inverse_kernel(cross_ref, table_ref, out_ref):
    depth = NB

    def rows(parity):
        groups = range(parity * GROUPS // PARITIES, (parity + 1) * GROUPS // PARITIES)
        parts = [
            jnp.concatenate([cross_ref[g, h, part] for g in groups for part in range(2)], axis=1)
            for h in range(SPLIT)
        ]
        return jnp.concatenate(parts, axis=0)

    a = jnp.dot(rows(0), table_ref[:depth], preferred_element_type=jnp.float32)
    b = jnp.dot(rows(1), table_ref[depth:], preferred_element_type=jnp.float32)
    out_ref[0, :, : LAGS // 2] = a + b
    out_ref[0, :, LAGS // 2 :] = a - b


def inverse(cross, scale):
    vmem = pl.BlockSpec(memory_space=pltpu.VMEM)
    return pl.pallas_call(
        inverse_kernel,
        in_specs=[vmem, vmem],
        out_specs=vmem,
        out_shape=jax.ShapeDtypeStruct((1, SPLIT * cross.shape[3], LAGS), jnp.float32),
        compiler_params=pltpu.CompilerParams(vmem_limit_bytes=16 * 2**20),
        name="inverse",
    )(cross, jnp.asarray(inverse_table(scale)))


def local(traces, pairs, block_row):
    _, channels, samples = traces.shape
    windows = samples // WIN
    parts, segs = lax.axis_size("pair"), lax.axis_size("seg")
    per_group = parts // (GROUPS * SPLIT)
    share = channels // segs // SPLIT
    width = BINS // per_group
    rows = 2 * windows * share + NOTE
    sent = whiten(pairs, block_row, traces[0], windows, segs)
    if per_group > 1:
        sent = sent.reshape(GROUPS, SPLIT, segs, rows, per_group, width).transpose(0, 4, 1, 2, 3, 5)
    sent = sent.reshape(parts * segs, rows, width)
    held = lax.all_to_all(sent, ("pair", "seg"), split_axis=0, concat_axis=0, tiled=True)
    cross_of = cross_groups if per_group == 1 else cross_narrow
    cross = cross_of(held.reshape(parts, segs, rows, width), windows, share)
    mine = lax.all_to_all(cross, "pair", split_axis=0, concat_axis=0, tiled=True)
    mine = mine.reshape(GROUPS, per_group, SPLIT, 2, share, width)
    mine = mine.transpose(0, 2, 3, 4, 1, 5).reshape(GROUPS, SPLIT, 2, share, BINS)
    return inverse(mine, 1.0 / (windows * segs))


def solution(mesh):
    placed = (P("pair", None, "seg"), P("pair", None), P())
    return jax.shard_map(
        local, mesh=mesh, in_specs=placed, out_specs=P("pair", "seg", None), check_vma=False
    )
```

```python
import functools

import jax
import jax.numpy as jnp
import ml_dtypes
import numpy as np
from jax import lax
from jax.experimental import pallas as pl
from jax.experimental.pallas import tpu as pltpu
from jax.sharding import PartitionSpec as P

WIN = 2048
NB = 512
LAGS = 2048
HALF = WIN // 2
BINS = 128
GROUPS = NB // BINS
SPLIT = 2
PARITIES = 2
NOTE = 8


def frequencies():
    even = np.arange(2, NB + 1, 2)
    odd = np.arange(1, NB + 1, 2)
    return np.concatenate((even, odd)).reshape(GROUPS, BINS)


def forward_table():
    phase = (frequencies()[:, :, None] * np.arange(HALF) % WIN) * (2.0 * np.pi / WIN)
    table = np.stack((np.cos(phase), -np.sin(phase)), axis=1).reshape(PARITIES, NB, HALF)
    return np.ascontiguousarray(table.transpose(0, 2, 1)).astype(ml_dtypes.bfloat16)


def inverse_table(scale):
    shifts = np.arange(LAGS // 2) - LAGS // 2
    phase = (frequencies()[:, :, None] * shifts % WIN) * (2.0 * np.pi / WIN)
    table = np.stack((np.cos(phase), -np.sin(phase)), axis=1) * scale
    return table.reshape(2 * NB, LAGS // 2).astype(ml_dtypes.bfloat16)


def whiten_kernel(windows, segs, pairs_hbm, row_hbm, traces_hbm, table_hbm, sent, pairs_ref, row_ref, frames, table, small_sem, frame_sem, table_sem):
    channels = frames.shape[1]
    share = channels // segs // SPLIT
    loads = [
        pltpu.make_async_copy(traces_hbm.at[:, pl.ds(w * WIN, WIN)], frames.at[w], frame_sem.at[w])
        for w in range(windows)
    ]
    tables = [
        pltpu.make_async_copy(table_hbm.at[i], table.at[i], table_sem.at[i]) for i in range(PARITIES)
    ]
    per = GROUPS // PARITIES
    small = [
        pltpu.make_async_copy(source, target, small_sem.at[k])
        for k, (source, target) in enumerate(((pairs_hbm, pairs_ref), (row_hbm, row_ref)))
    ]
    tables[0].start()
    for load in loads:
        load.start()
    tables[1].start()
    for load in small:
        load.start()
    for load in loads:
        load.wait()
    for load in small:
        load.wait()
    first_row = row_ref[pairs_ref[0, 0]].astype(jnp.float32)
    second_row = row_ref[pairs_ref[0, 1]].astype(jnp.float32)
    line = lax.broadcasted_iota(jnp.int32, (NOTE, BINS), 0)
    note = jnp.where(line == 0, first_row, second_row).astype(jnp.bfloat16)
    sent[:, :, :, 2 * windows * share :] = jnp.broadcast_to(note, (GROUPS, SPLIT, segs, NOTE, BINS))
    for i in range(PARITIES):
        tables[i].wait()
        for w in range(windows):
            halves = jnp.concatenate((frames[w, :, :HALF], frames[w, :, HALF:]), axis=0)
            product = jnp.dot(halves, table[i], preferred_element_type=jnp.float32)
            first, second = product[:channels], product[channels:]
            spectra = first + second if i == 0 else first - second
            for k in range(per):
                real = spectra[:, 2 * k * BINS : (2 * k + 1) * BINS]
                imag = spectra[:, (2 * k + 1) * BINS : (2 * k + 2) * BINS]
                power = jnp.sum(real * real + imag * imag, axis=0, keepdims=True) * (1.0 / channels)
                gain = lax.rsqrt(power + 1e-06)
                for part, values in enumerate((real, imag)):
                    white = (values * gain).astype(jnp.bfloat16).reshape(segs, SPLIT, share, BINS)
                    at = (2 * w + part) * share
                    for h in range(SPLIT):
                        sent[i * per + k, h, :, at : at + share] = white[:, h]


def in_hbm(values):
    return pltpu.with_memory_space_constraint(values, pltpu.HBM)


def whiten(pairs, block_row, traces, windows, segs):
    channels = traces.shape[0]
    share = channels // segs // SPLIT
    shape = (GROUPS, SPLIT, segs, 2 * windows * share + NOTE, BINS)
    hbm = pl.BlockSpec(memory_space=pl.ANY)
    return pl.pallas_call(
        functools.partial(whiten_kernel, windows, segs),
        in_specs=[hbm, hbm, hbm, hbm],
        out_specs=pl.BlockSpec(memory_space=pltpu.VMEM),
        out_shape=pltpu.VMEM(shape, jnp.bfloat16),
        scratch_shapes=[
            pltpu.SMEM(pairs.shape, jnp.int32),
            pltpu.SMEM(block_row.shape, jnp.int32),
            pltpu.VMEM((windows, channels, WIN), jnp.bfloat16),
            pltpu.VMEM((PARITIES, HALF, NB), jnp.bfloat16),
            pltpu.SemaphoreType.DMA((2,)),
            pltpu.SemaphoreType.DMA((windows,)),
            pltpu.SemaphoreType.DMA((PARITIES,)),
        ],
        compiler_params=pltpu.CompilerParams(vmem_limit_bytes=24 * 2**20),
        name="whiten",
    )(*(in_hbm(values) for values in (pairs, block_row, traces, jnp.asarray(forward_table()))))


def cross_kernel(windows, spectra_ref, out_ref):
    segs = spectra_ref.shape[1]
    share = out_ref.shape[2]
    notes = [spectra_ref[i, 0, 2 * windows * share :].astype(jnp.float32) for i in range(out_ref.shape[0])]
    rows = [(note[0, 0].astype(jnp.int32), note[1, 0].astype(jnp.int32)) for note in notes]
    for i, (a, b) in enumerate(rows):
        real = jnp.zeros(out_ref.shape[2:], jnp.float32)
        imag = jnp.zeros(out_ref.shape[2:], jnp.float32)
        for s in range(segs):
            for w in range(windows):
                re = slice(2 * w * share, (2 * w + 1) * share)
                im = slice((2 * w + 1) * share, (2 * w + 2) * share)
                first_re = spectra_ref[a, s, re].astype(jnp.float32)
                first_im = spectra_ref[a, s, im].astype(jnp.float32)
                second_re = spectra_ref[b, s, re].astype(jnp.float32)
                second_im = spectra_ref[b, s, im].astype(jnp.float32)
                real += first_re * second_re + first_im * second_im
                imag += first_re * second_im - first_im * second_re
        out_ref[i, 0] = real.astype(jnp.bfloat16)
        out_ref[i, 1] = imag.astype(jnp.bfloat16)


def cross_groups(spectra, windows, share):
    vmem = pl.BlockSpec(memory_space=pltpu.VMEM)
    return pl.pallas_call(
        functools.partial(cross_kernel, windows),
        in_specs=[vmem],
        out_specs=vmem,
        out_shape=jax.ShapeDtypeStruct((spectra.shape[0], 2, share, BINS), jnp.bfloat16),
        compiler_params=pltpu.CompilerParams(vmem_limit_bytes=8 * 2**20),
        name="cross",
    )(spectra)


def cross_narrow(spectra, windows, share):
    parts, segs, rows, width = spectra.shape
    noted = spectra[:, 0, rows - NOTE : rows - NOTE + 2, 0].astype(jnp.int32)
    parted = spectra[:, :, : rows - NOTE].reshape(parts, segs * windows, 2, share, width)
    first = parted[noted[:, 0]].astype(jnp.float32)
    second = parted[noted[:, 1]].astype(jnp.float32)
    real = jnp.sum(first[:, :, 0] * second[:, :, 0] + first[:, :, 1] * second[:, :, 1], axis=1)
    imag = jnp.sum(first[:, :, 0] * second[:, :, 1] - first[:, :, 1] * second[:, :, 0], axis=1)
    return jnp.stack((real, imag), axis=1).astype(jnp.bfloat16)


def inverse_kernel(cross_ref, table_ref, out_ref):
    depth = NB

    def rows(parity):
        groups = range(parity * GROUPS // PARITIES, (parity + 1) * GROUPS // PARITIES)
        parts = [
            jnp.concatenate([cross_ref[g, h, part] for g in groups for part in range(2)], axis=1)
            for h in range(SPLIT)
        ]
        return jnp.concatenate(parts, axis=0)

    a = jnp.dot(rows(0), table_ref[:depth], preferred_element_type=jnp.float32)
    b = jnp.dot(rows(1), table_ref[depth:], preferred_element_type=jnp.float32)
    out_ref[0, :, : LAGS // 2] = a + b
    out_ref[0, :, LAGS // 2 :] = a - b


def inverse(cross, scale):
    vmem = pl.BlockSpec(memory_space=pltpu.VMEM)
    return pl.pallas_call(
        inverse_kernel,
        in_specs=[vmem, vmem],
        out_specs=vmem,
        out_shape=jax.ShapeDtypeStruct((1, SPLIT * cross.shape[3], LAGS), jnp.float32),
        compiler_params=pltpu.CompilerParams(vmem_limit_bytes=16 * 2**20),
        name="inverse",
    )(cross, jnp.asarray(inverse_table(scale)))


def local(traces, pairs, block_row):
    _, channels, samples = traces.shape
    windows = samples // WIN
    parts, segs = lax.axis_size("pair"), lax.axis_size("seg")
    per_group = parts // (GROUPS * SPLIT)
    share = channels // segs // SPLIT
    width = BINS // per_group
    rows = 2 * windows * share + NOTE
    sent = whiten(pairs, block_row, traces[0], windows, segs)
    if per_group > 1:
        sent = sent.reshape(GROUPS, SPLIT, segs, rows, per_group, width).transpose(0, 4, 1, 2, 3, 5)
    sent = sent.reshape(parts * segs, rows, width)
    held = lax.all_to_all(sent, ("pair", "seg"), split_axis=0, concat_axis=0, tiled=True)
    cross_of = cross_groups if per_group == 1 else cross_narrow
    cross = cross_of(held.reshape(parts, segs, rows, width), windows, share)
    mine = lax.all_to_all(cross, "pair", split_axis=0, concat_axis=0, tiled=True)
    mine = mine.reshape(GROUPS, per_group, SPLIT, 2, share, width)
    mine = mine.transpose(0, 2, 3, 4, 1, 5).reshape(GROUPS, SPLIT, 2, share, BINS)
    return inverse(mine, 1.0 / (windows * segs))


def solution(mesh):
    placed = (P("pair", None, "seg"), P("pair", None), P())
    return jax.shard_map(
        local, mesh=mesh, in_specs=placed, out_specs=P("pair", "seg", None), check_vma=False
    )
```

```python
import functools

import jax
import jax.numpy as jnp
import ml_dtypes
import numpy as np
from jax import lax
from jax.experimental import pallas as pl
from jax.experimental.pallas import tpu as pltpu
from jax.sharding import PartitionSpec as P

WIN = 2048
NB = 512
LAGS = 2048
HALF = WIN // 2
BINS = 128
GROUPS = NB // BINS
SPLIT = 2
PARITIES = 2
NOTE = 8


def frequencies():
    even = np.arange(2, NB + 1, 2)
    odd = np.arange(1, NB + 1, 2)
    return np.concatenate((even, odd)).reshape(GROUPS, BINS)


def forward_table():
    phase = (frequencies()[:, :, None] * np.arange(HALF) % WIN) * (2.0 * np.pi / WIN)
    table = np.stack((np.cos(phase), -np.sin(phase)), axis=1).reshape(PARITIES, NB, HALF)
    return np.ascontiguousarray(table.transpose(0, 2, 1)).astype(ml_dtypes.bfloat16)


def inverse_table(scale):
    shifts = np.arange(LAGS // 2) - LAGS // 2
    phase = (frequencies()[:, :, None] * shifts % WIN) * (2.0 * np.pi / WIN)
    table = np.stack((np.cos(phase), -np.sin(phase)), axis=1) * scale
    return table.reshape(2 * NB, LAGS // 2).astype(ml_dtypes.bfloat16)


def whiten_kernel(windows, segs, pairs_hbm, row_hbm, traces_hbm, table_hbm, sent, pairs_ref, row_ref, frames, table, small_sem, frame_sem, table_sem):
    channels = frames.shape[1]
    share = channels // segs // SPLIT
    loads = [
        pltpu.make_async_copy(traces_hbm.at[:, pl.ds(w * WIN, WIN)], frames.at[w], frame_sem.at[w])
        for w in range(windows)
    ]
    tables = [
        pltpu.make_async_copy(table_hbm.at[i], table.at[i], table_sem.at[i]) for i in range(PARITIES)
    ]
    small = [
        pltpu.make_async_copy(source, target, small_sem.at[k])
        for k, (source, target) in enumerate(((pairs_hbm, pairs_ref), (row_hbm, row_ref)))
    ]
    per = GROUPS // PARITIES
    tables[0].start()
    for load in loads:
        load.start()
    tables[1].start()
    for load in small:
        load.start()

    def one(w, i):
        halves = jnp.concatenate((frames[w, :, :HALF], frames[w, :, HALF:]), axis=0)
        product = jnp.dot(halves, table[i], preferred_element_type=jnp.float32)
        first, second = product[:channels], product[channels:]
        spectra = first + second if i == 0 else first - second
        for k in range(per):
            real = spectra[:, 2 * k * BINS : (2 * k + 1) * BINS]
            imag = spectra[:, (2 * k + 1) * BINS : (2 * k + 2) * BINS]
            power = jnp.sum(real * real + imag * imag, axis=0, keepdims=True) * (1.0 / channels)
            gain = lax.rsqrt(power + 1e-06)
            for part, values in enumerate((real, imag)):
                white = (values * gain).astype(jnp.bfloat16).reshape(segs, SPLIT, share, BINS)
                at = (2 * w + part) * share
                for h in range(SPLIT):
                    sent[i * per + k, h, :, at : at + share] = white[:, h]

    early = windows // 2
    tables[0].wait()
    for w in range(early):
        loads[w].wait()
    for w in range(early):
        one(w, 0)
    for w in range(early, windows):
        loads[w].wait()
    tables[1].wait()
    for load in small:
        load.wait()
    parts = row_ref.shape[0]
    first_row = ((row_ref[pairs_ref[0, 0]] + parts // 2) % parts).astype(jnp.float32)
    second_row = ((row_ref[pairs_ref[0, 1]] + parts // 2) % parts).astype(jnp.float32)
    line = lax.broadcasted_iota(jnp.int32, (NOTE, BINS), 0)
    note = jnp.where(line == 0, first_row, second_row).astype(jnp.bfloat16)
    sent[:, :, :, 2 * windows * share :] = jnp.broadcast_to(note, (GROUPS, SPLIT, segs, NOTE, BINS))
    for w in range(early, windows):
        one(w, 0)
    for w in range(windows):
        one(w, 1)


def in_hbm(values):
    return pltpu.with_memory_space_constraint(values, pltpu.HBM)


def whiten(pairs, block_row, traces, windows, segs):
    channels = traces.shape[0]
    share = channels // segs // SPLIT
    shape = (GROUPS, SPLIT, segs, 2 * windows * share + NOTE, BINS)
    hbm = pl.BlockSpec(memory_space=pl.ANY)
    return pl.pallas_call(
        functools.partial(whiten_kernel, windows, segs),
        in_specs=[hbm, hbm, hbm, hbm],
        out_specs=pl.BlockSpec(memory_space=pltpu.VMEM),
        out_shape=pltpu.VMEM(shape, jnp.bfloat16),
        scratch_shapes=[
            pltpu.SMEM(pairs.shape, jnp.int32),
            pltpu.SMEM(block_row.shape, jnp.int32),
            pltpu.VMEM((windows, channels, WIN), jnp.bfloat16),
            pltpu.VMEM((PARITIES, HALF, NB), jnp.bfloat16),
            pltpu.SemaphoreType.DMA((2,)),
            pltpu.SemaphoreType.DMA((windows,)),
            pltpu.SemaphoreType.DMA((PARITIES,)),
        ],
        compiler_params=pltpu.CompilerParams(vmem_limit_bytes=24 * 2**20),
        name="whiten",
    )(*(in_hbm(values) for values in (pairs, block_row, traces, jnp.asarray(forward_table()))))


def cross_kernel(windows, spectra_ref, out_ref):
    segs = spectra_ref.shape[1]
    share = out_ref.shape[2]
    notes = [spectra_ref[i, 0, 2 * windows * share :].astype(jnp.float32) for i in range(out_ref.shape[0])]
    rows = [(note[0, 0].astype(jnp.int32), note[1, 0].astype(jnp.int32)) for note in notes]
    for i, (a, b) in enumerate(rows):
        real = jnp.zeros(out_ref.shape[2:], jnp.float32)
        imag = jnp.zeros(out_ref.shape[2:], jnp.float32)
        for s in range(segs):
            for w in range(windows):
                re = slice(2 * w * share, (2 * w + 1) * share)
                im = slice((2 * w + 1) * share, (2 * w + 2) * share)
                first_re = spectra_ref[a, s, re].astype(jnp.float32)
                first_im = spectra_ref[a, s, im].astype(jnp.float32)
                second_re = spectra_ref[b, s, re].astype(jnp.float32)
                second_im = spectra_ref[b, s, im].astype(jnp.float32)
                real += first_re * second_re + first_im * second_im
                imag += first_re * second_im - first_im * second_re
        out_ref[i, 0] = real.astype(jnp.bfloat16)
        out_ref[i, 1] = imag.astype(jnp.bfloat16)


def cross_groups(spectra, windows, share):
    vmem = pl.BlockSpec(memory_space=pltpu.VMEM)
    return pl.pallas_call(
        functools.partial(cross_kernel, windows),
        in_specs=[vmem],
        out_specs=vmem,
        out_shape=jax.ShapeDtypeStruct((spectra.shape[0], 2, share, BINS), jnp.bfloat16),
        compiler_params=pltpu.CompilerParams(vmem_limit_bytes=8 * 2**20),
        name="cross",
    )(spectra)


def cross_narrow(spectra, windows, share):
    parts, segs, rows, width = spectra.shape
    noted = spectra[:, 0, rows - NOTE : rows - NOTE + 2, 0].astype(jnp.int32)
    parted = spectra[:, :, : rows - NOTE].reshape(parts, segs * windows, 2, share, width)
    first = parted[noted[:, 0]].astype(jnp.float32)
    second = parted[noted[:, 1]].astype(jnp.float32)
    real = jnp.sum(first[:, :, 0] * second[:, :, 0] + first[:, :, 1] * second[:, :, 1], axis=1)
    imag = jnp.sum(first[:, :, 0] * second[:, :, 1] - first[:, :, 1] * second[:, :, 0], axis=1)
    return jnp.stack((real, imag), axis=1).astype(jnp.bfloat16)


def inverse_kernel(cross_ref, table_ref, out_ref):
    depth = NB

    def rows(parity):
        groups = range(parity * GROUPS // PARITIES, (parity + 1) * GROUPS // PARITIES)
        parts = [
            jnp.concatenate([cross_ref[g, h, part] for g in groups for part in range(2)], axis=1)
            for h in range(SPLIT)
        ]
        return jnp.concatenate(parts, axis=0)

    a = jnp.dot(rows(0), table_ref[:depth], preferred_element_type=jnp.float32)
    b = jnp.dot(rows(1), table_ref[depth:], preferred_element_type=jnp.float32)
    out_ref[0, :, : LAGS // 2] = a + b
    out_ref[0, :, LAGS // 2 :] = a - b


def inverse(cross, scale):
    vmem = pl.BlockSpec(memory_space=pltpu.VMEM)
    return pl.pallas_call(
        inverse_kernel,
        in_specs=[vmem, vmem],
        out_specs=vmem,
        out_shape=jax.ShapeDtypeStruct((1, SPLIT * cross.shape[3], LAGS), jnp.float32),
        compiler_params=pltpu.CompilerParams(vmem_limit_bytes=16 * 2**20),
        name="inverse",
    )(cross, jnp.asarray(inverse_table(scale)))


def exchange_order(parts):
    return [(i + parts // 2) % parts for i in range(parts)]


def local(traces, pairs, block_row):
    _, channels, samples = traces.shape
    windows = samples // WIN
    parts, segs = lax.axis_size("pair"), lax.axis_size("seg")
    per_group = parts // (GROUPS * SPLIT)
    share = channels // segs // SPLIT
    width = BINS // per_group
    rows = 2 * windows * share + NOTE
    sent = whiten(pairs, block_row, traces[0], windows, segs)
    if per_group > 1:
        sent = sent.reshape(GROUPS, SPLIT, segs, rows, per_group, width).transpose(0, 4, 1, 2, 3, 5)
    sent = sent.reshape(parts * segs, rows, width)
    order = exchange_order(parts)
    everyone = [i * segs + s for i in order for s in range(segs)]
    held = lax.all_to_all(
        sent, ("pair", "seg"), split_axis=0, concat_axis=0, tiled=True, axis_index_groups=[everyone]
    )
    cross_of = cross_groups if per_group == 1 else cross_narrow
    cross = cross_of(held.reshape(parts, segs, rows, width), windows, share)
    mine = lax.all_to_all(
        cross, "pair", split_axis=0, concat_axis=0, tiled=True, axis_index_groups=[order]
    )
    mine = mine.reshape(GROUPS, per_group, SPLIT, 2, share, width)
    mine = mine.transpose(0, 2, 3, 4, 1, 5).reshape(GROUPS, SPLIT, 2, share, BINS)
    return inverse(mine, 1.0 / (windows * segs))


def solution(mesh):
    placed = (P("pair", None, "seg"), P("pair", None), P())
    return jax.shard_map(
        local, mesh=mesh, in_specs=placed, out_specs=P("pair", "seg", None), check_vma=False
    )
```

```python
import functools

import jax
import jax.numpy as jnp
import ml_dtypes
import numpy as np
from jax import lax
from jax.experimental import pallas as pl
from jax.experimental.pallas import tpu as pltpu
from jax.sharding import PartitionSpec as P

WIN = 2048
NB = 512
LAGS = 2048
HALF = WIN // 2
BINS = 128
GROUPS = NB // BINS
SPLIT = 2
PARITIES = 2
NOTE = 8
NEAR = 2


def frequencies():
    even = np.arange(2, NB + 1, 2)
    odd = np.arange(1, NB + 1, 2)
    return np.concatenate((even, odd)).reshape(GROUPS, BINS)


def forward_table():
    phase = (frequencies()[:, :, None] * np.arange(HALF) % WIN) * (2.0 * np.pi / WIN)
    table = np.stack((np.cos(phase), -np.sin(phase)), axis=1).reshape(PARITIES, NB, HALF)
    return np.ascontiguousarray(table.transpose(0, 2, 1)).astype(ml_dtypes.bfloat16)


def inverse_table(scale):
    shifts = np.arange(LAGS // 2) - LAGS // 2
    phase = (frequencies()[:, :, None] * shifts % WIN) * (2.0 * np.pi / WIN)
    table = np.stack((np.cos(phase), -np.sin(phase)), axis=1) * scale
    return table.reshape(2 * NB, LAGS // 2).astype(ml_dtypes.bfloat16)


def whiten_kernel(windows, far, near, pairs_hbm, row_hbm, traces_hbm, table_hbm, sent, pairs_ref, row_ref, frames, table, small_sem, frame_sem, table_sem):
    channels = frames.shape[1]
    share = channels // (far * near * SPLIT)
    loads = [
        pltpu.make_async_copy(traces_hbm.at[:, pl.ds(w * WIN, WIN)], frames.at[w], frame_sem.at[w])
        for w in range(windows)
    ]
    tables = [
        pltpu.make_async_copy(table_hbm.at[i], table.at[i], table_sem.at[i]) for i in range(PARITIES)
    ]
    small = [
        pltpu.make_async_copy(source, target, small_sem.at[k])
        for k, (source, target) in enumerate(((pairs_hbm, pairs_ref), (row_hbm, row_ref)))
    ]
    per = GROUPS // PARITIES
    tables[0].start()
    for load in loads:
        load.start()
    tables[1].start()
    for load in small:
        load.start()

    def one(w, i):
        halves = jnp.concatenate((frames[w, :, :HALF], frames[w, :, HALF:]), axis=0)
        product = jnp.dot(halves, table[i], preferred_element_type=jnp.float32)
        first, second = product[:channels], product[channels:]
        spectra = first + second if i == 0 else first - second
        for k in range(per):
            real = spectra[:, 2 * k * BINS : (2 * k + 1) * BINS]
            imag = spectra[:, (2 * k + 1) * BINS : (2 * k + 2) * BINS]
            power = jnp.sum(real * real + imag * imag, axis=0, keepdims=True) * (1.0 / channels)
            gain = lax.rsqrt(power + 1e-06)
            for part, values in enumerate((real, imag)):
                white = (values * gain).astype(jnp.bfloat16).reshape(far, near, SPLIT, share, BINS)
                for f in range(far):
                    at = (2 * (f * windows + w) + part) * share
                    for h in range(SPLIT):
                        sent[i * per + k, h, :, at : at + share] = white[f, :, h]

    early = windows // 2
    tables[0].wait()
    for w in range(early):
        loads[w].wait()
    for w in range(early):
        one(w, 0)
    for w in range(early, windows):
        loads[w].wait()
    tables[1].wait()
    for load in small:
        load.wait()
    parts = row_ref.shape[0]
    first_row = ((row_ref[pairs_ref[0, 0]] + parts // 2) % parts).astype(jnp.float32)
    second_row = ((row_ref[pairs_ref[0, 1]] + parts // 2) % parts).astype(jnp.float32)
    line = lax.broadcasted_iota(jnp.int32, (NOTE, BINS), 0)
    note = jnp.where(line == 0, first_row, second_row).astype(jnp.bfloat16)
    sent[:, :, :, 2 * far * windows * share :] = jnp.broadcast_to(note, (GROUPS, SPLIT, near, NOTE, BINS))
    for w in range(early, windows):
        one(w, 0)
    for w in range(windows):
        one(w, 1)


def in_hbm(values):
    return pltpu.with_memory_space_constraint(values, pltpu.HBM)


def whiten(pairs, block_row, traces, windows, far, near):
    channels = traces.shape[0]
    share = channels // (far * near * SPLIT)
    shape = (GROUPS, SPLIT, near, 2 * far * windows * share + NOTE, BINS)
    hbm = pl.BlockSpec(memory_space=pl.ANY)
    return pl.pallas_call(
        functools.partial(whiten_kernel, windows, far, near),
        in_specs=[hbm, hbm, hbm, hbm],
        out_specs=pl.BlockSpec(memory_space=pltpu.VMEM),
        out_shape=pltpu.VMEM(shape, jnp.bfloat16),
        scratch_shapes=[
            pltpu.SMEM(pairs.shape, jnp.int32),
            pltpu.SMEM(block_row.shape, jnp.int32),
            pltpu.VMEM((windows, channels, WIN), jnp.bfloat16),
            pltpu.VMEM((PARITIES, HALF, NB), jnp.bfloat16),
            pltpu.SemaphoreType.DMA((2,)),
            pltpu.SemaphoreType.DMA((windows,)),
            pltpu.SemaphoreType.DMA((PARITIES,)),
        ],
        compiler_params=pltpu.CompilerParams(vmem_limit_bytes=24 * 2**20),
        name="whiten",
    )(*(in_hbm(values) for values in (pairs, block_row, traces, jnp.asarray(forward_table()))))


def cross_kernel(windows, spectra_ref, out_ref):
    count, far, _, share, _ = out_ref.shape
    near = spectra_ref.shape[1]
    notes = [spectra_ref[i, 0, 2 * far * windows * share :].astype(jnp.float32) for i in range(count)]
    rows = [(note[0, 0].astype(jnp.int32), note[1, 0].astype(jnp.int32)) for note in notes]
    for i, (a, b) in enumerate(rows):
        for f in range(far):
            real = jnp.zeros(out_ref.shape[3:], jnp.float32)
            imag = jnp.zeros(out_ref.shape[3:], jnp.float32)
            for n in range(near):
                for w in range(windows):
                    at = 2 * (f * windows + w) * share
                    re, im = slice(at, at + share), slice(at + share, at + 2 * share)
                    first_re = spectra_ref[a, n, re].astype(jnp.float32)
                    first_im = spectra_ref[a, n, im].astype(jnp.float32)
                    second_re = spectra_ref[b, n, re].astype(jnp.float32)
                    second_im = spectra_ref[b, n, im].astype(jnp.float32)
                    real += first_re * second_re + first_im * second_im
                    imag += first_re * second_im - first_im * second_re
            out_ref[i, f, 0] = real.astype(jnp.bfloat16)
            out_ref[i, f, 1] = imag.astype(jnp.bfloat16)


def cross_groups(spectra, windows, far, share):
    vmem = pl.BlockSpec(memory_space=pltpu.VMEM)
    return pl.pallas_call(
        functools.partial(cross_kernel, windows),
        in_specs=[vmem],
        out_specs=vmem,
        out_shape=jax.ShapeDtypeStruct((spectra.shape[0], far, 2, share, BINS), jnp.bfloat16),
        compiler_params=pltpu.CompilerParams(vmem_limit_bytes=8 * 2**20),
        name="cross",
    )(spectra)


def cross_narrow(spectra, windows, far, share):
    parts, near, rows, width = spectra.shape
    noted = spectra[:, 0, rows - NOTE : rows - NOTE + 2, 0].astype(jnp.int32)
    parted = spectra[:, :, : rows - NOTE].reshape(parts, near, far, windows, 2, share, width)
    first = parted[noted[:, 0]].astype(jnp.float32)
    second = parted[noted[:, 1]].astype(jnp.float32)
    first_re, first_im, second_re, second_im = first[..., 0, :, :], first[..., 1, :, :], second[..., 0, :, :], second[..., 1, :, :]
    real = jnp.sum(first_re * second_re + first_im * second_im, axis=(1, 3))
    imag = jnp.sum(first_re * second_im - first_im * second_re, axis=(1, 3))
    return jnp.stack((real, imag), axis=2).astype(jnp.bfloat16)


def inverse_kernel(cross_ref, table_ref, out_ref):
    depth = NB
    far, share = cross_ref.shape[2], cross_ref.shape[4]

    def lags(parity):
        groups = range(parity * GROUPS // PARITIES, (parity + 1) * GROUPS // PARITIES)
        parts = [
            jnp.concatenate([cross_ref[g, h, f, part] for g in groups for part in range(2)], axis=1)
            for f in range(far)
            for h in range(SPLIT)
        ]
        table = table_ref[parity * depth : (parity + 1) * depth]
        product = jnp.dot(jnp.concatenate(parts, axis=0), table, preferred_element_type=jnp.float32)
        return sum(product[f * SPLIT * share : (f + 1) * SPLIT * share] for f in range(far))

    a, b = lags(0), lags(1)
    out_ref[0, :, : LAGS // 2] = a + b
    out_ref[0, :, LAGS // 2 :] = a - b


def inverse(cross, scale):
    vmem = pl.BlockSpec(memory_space=pltpu.VMEM)
    return pl.pallas_call(
        inverse_kernel,
        in_specs=[vmem, vmem],
        out_specs=vmem,
        out_shape=jax.ShapeDtypeStruct((1, SPLIT * cross.shape[4], LAGS), jnp.float32),
        compiler_params=pltpu.CompilerParams(vmem_limit_bytes=16 * 2**20),
        name="inverse",
    )(cross, jnp.asarray(inverse_table(scale)))


def exchange_order(parts):
    return [(i + parts // 2) % parts for i in range(parts)]


def all_to_all(sent, order, axis):
    size = lax.axis_size(axis)
    group = [i * size + k for i in order for k in range(size)]
    return lax.all_to_all(
        sent, ("pair", axis), split_axis=0, concat_axis=0, tiled=True, axis_index_groups=[group]
    )


def local(traces, pairs, block_row):
    _, channels, samples = traces.shape
    windows = samples // WIN
    parts, far, near = lax.axis_size("pair"), lax.axis_size("far"), lax.axis_size("near")
    per_group = parts // (GROUPS * SPLIT)
    share = channels // (far * near * SPLIT)
    width = BINS // per_group
    rows = 2 * far * windows * share + NOTE
    sent = whiten(pairs, block_row, traces[0], windows, far, near)
    if per_group > 1:
        sent = sent.reshape(GROUPS, SPLIT, near, rows, per_group, width).transpose(0, 4, 1, 2, 3, 5)
    order = exchange_order(parts)
    held = all_to_all(sent.reshape(parts * near, rows, width), order, "near")
    cross_of = cross_groups if per_group == 1 else cross_narrow
    cross = cross_of(held.reshape(parts, near, rows, width), windows, far, share)
    mine = all_to_all(cross.reshape(parts * far, 2, share, width), order, "far")
    mine = mine.reshape(GROUPS, per_group, SPLIT, far, 2, share, width)
    mine = mine.transpose(0, 2, 3, 4, 5, 1, 6).reshape(GROUPS, SPLIT, far, 2, share, BINS)
    return inverse(mine, 1.0 / (windows * far * near))


def solution(mesh):
    pairs, segs = mesh.devices.shape
    split = jax.sharding.Mesh(mesh.devices.reshape(pairs, segs // NEAR, NEAR), ("pair", "far", "near"))
    placed = (P("pair", None, ("far", "near")), P("pair", None), P())
    return jax.shard_map(
        local, mesh=split, in_specs=placed, out_specs=P("pair", ("far", "near"), None), check_vma=False
    )
```

```python
import functools

import jax
import jax.numpy as jnp
import ml_dtypes
import numpy as np
from jax import lax
from jax.experimental import pallas as pl
from jax.experimental.pallas import tpu as pltpu
from jax.sharding import PartitionSpec as P

WIN = 2048
NB = 512
LAGS = 2048
HALF = WIN // 2
BINS = 128
GROUPS = NB // BINS
SPLIT = 2
PARITIES = 2
NOTE = 8
NEAR = 2


def frequencies():
    even = np.arange(2, NB + 1, 2)
    odd = np.arange(1, NB + 1, 2)
    return np.concatenate((even, odd)).reshape(GROUPS, BINS)


def forward_table():
    phase = (frequencies()[:, :, None] * np.arange(HALF) % WIN) * (2.0 * np.pi / WIN)
    table = np.stack((np.cos(phase), -np.sin(phase)), axis=1).reshape(PARITIES, NB, HALF)
    return np.ascontiguousarray(table.transpose(0, 2, 1)).astype(ml_dtypes.bfloat16)


def inverse_table(scale):
    shifts = np.arange(LAGS // 2) - LAGS // 2
    phase = (frequencies()[:, :, None] * shifts % WIN) * (2.0 * np.pi / WIN)
    table = np.stack((np.cos(phase), -np.sin(phase)), axis=1) * scale
    return table.reshape(2 * NB, LAGS // 2).astype(ml_dtypes.bfloat16)


def whiten_kernel(windows, far, near, pairs_hbm, row_hbm, traces_hbm, table_hbm, sent, pairs_ref, row_ref, frames, table, small_sem, frame_sem, table_sem):
    channels = frames.shape[1]
    share = channels // (far * near * SPLIT)
    loads = [
        pltpu.make_async_copy(traces_hbm.at[:, pl.ds(w * WIN, WIN)], frames.at[w], frame_sem.at[w])
        for w in range(windows)
    ]
    tables = [
        pltpu.make_async_copy(table_hbm.at[i], table.at[i], table_sem.at[i]) for i in range(PARITIES)
    ]
    small = [
        pltpu.make_async_copy(source, target, small_sem.at[k])
        for k, (source, target) in enumerate(((pairs_hbm, pairs_ref), (row_hbm, row_ref)))
    ]
    per = GROUPS // PARITIES
    tables[0].start()
    for load in loads:
        load.start()
    tables[1].start()
    for load in small:
        load.start()

    def one(w, i):
        halves = jnp.concatenate((frames[w, :, :HALF], frames[w, :, HALF:]), axis=0)
        product = jnp.dot(halves, table[i], preferred_element_type=jnp.float32)
        first, second = product[:channels], product[channels:]
        spectra = first + second if i == 0 else first - second
        for k in range(per):
            real = spectra[:, 2 * k * BINS : (2 * k + 1) * BINS]
            imag = spectra[:, (2 * k + 1) * BINS : (2 * k + 2) * BINS]
            power = jnp.sum(real * real + imag * imag, axis=0, keepdims=True) * (1.0 / channels)
            gain = lax.rsqrt(power + 1e-06)
            for part, values in enumerate((real, imag)):
                white = (values * gain).astype(jnp.bfloat16).reshape(far, near, SPLIT, share, BINS)
                for f in range(far):
                    at = (2 * (f * windows + w) + part) * share
                    for h in range(SPLIT):
                        for n in range(near):
                            sent[i * per + k, h, near - 1 - n, at : at + share] = white[f, n, h]

    early = windows // 2
    tables[0].wait()
    for w in range(early):
        loads[w].wait()
    for w in range(early):
        one(w, 0)
    for w in range(early, windows):
        loads[w].wait()
    tables[1].wait()
    for load in small:
        load.wait()
    turn = row_ref.shape[0] // 2 + 1
    first_row = (row_ref[pairs_ref[0, 0]] ^ turn).astype(jnp.float32)
    second_row = (row_ref[pairs_ref[0, 1]] ^ turn).astype(jnp.float32)
    line = lax.broadcasted_iota(jnp.int32, (NOTE, BINS), 0)
    note = jnp.where(line == 0, first_row, second_row).astype(jnp.bfloat16)
    sent[:, :, :, 2 * far * windows * share :] = jnp.broadcast_to(note, (GROUPS, SPLIT, near, NOTE, BINS))
    for w in range(early, windows):
        one(w, 0)
    for w in range(windows):
        one(w, 1)


def in_hbm(values):
    return pltpu.with_memory_space_constraint(values, pltpu.HBM)


def whiten(pairs, block_row, traces, windows, far, near):
    channels = traces.shape[0]
    share = channels // (far * near * SPLIT)
    shape = (GROUPS, SPLIT, near, 2 * far * windows * share + NOTE, BINS)
    hbm = pl.BlockSpec(memory_space=pl.ANY)
    return pl.pallas_call(
        functools.partial(whiten_kernel, windows, far, near),
        in_specs=[hbm, hbm, hbm, hbm],
        out_specs=pl.BlockSpec(memory_space=pltpu.VMEM),
        out_shape=pltpu.VMEM(shape, jnp.bfloat16),
        scratch_shapes=[
            pltpu.SMEM(pairs.shape, jnp.int32),
            pltpu.SMEM(block_row.shape, jnp.int32),
            pltpu.VMEM((windows, channels, WIN), jnp.bfloat16),
            pltpu.VMEM((PARITIES, HALF, NB), jnp.bfloat16),
            pltpu.SemaphoreType.DMA((2,)),
            pltpu.SemaphoreType.DMA((windows,)),
            pltpu.SemaphoreType.DMA((PARITIES,)),
        ],
        compiler_params=pltpu.CompilerParams(vmem_limit_bytes=24 * 2**20),
        name="whiten",
    )(*(in_hbm(values) for values in (pairs, block_row, traces, jnp.asarray(forward_table()))))


def cross_kernel(windows, spectra_ref, out_ref):
    count, far, _, share, _ = out_ref.shape
    near = spectra_ref.shape[1]
    notes = [spectra_ref[i, 0, 2 * far * windows * share :].astype(jnp.float32) for i in range(count)]
    rows = [(note[0, 0].astype(jnp.int32), note[1, 0].astype(jnp.int32)) for note in notes]
    for i, (a, b) in enumerate(rows):
        for f in range(far):
            real = jnp.zeros(out_ref.shape[3:], jnp.float32)
            imag = jnp.zeros(out_ref.shape[3:], jnp.float32)
            for n in range(near):
                for w in range(windows):
                    at = 2 * (f * windows + w) * share
                    re, im = slice(at, at + share), slice(at + share, at + 2 * share)
                    first_re = spectra_ref[a, n, re].astype(jnp.float32)
                    first_im = spectra_ref[a, n, im].astype(jnp.float32)
                    second_re = spectra_ref[b, n, re].astype(jnp.float32)
                    second_im = spectra_ref[b, n, im].astype(jnp.float32)
                    real += first_re * second_re + first_im * second_im
                    imag += first_re * second_im - first_im * second_re
            out_ref[i, far - 1 - f, 0] = real.astype(jnp.bfloat16)
            out_ref[i, far - 1 - f, 1] = imag.astype(jnp.bfloat16)


def cross_groups(spectra, windows, far, share):
    vmem = pl.BlockSpec(memory_space=pltpu.VMEM)
    return pl.pallas_call(
        functools.partial(cross_kernel, windows),
        in_specs=[vmem],
        out_specs=vmem,
        out_shape=jax.ShapeDtypeStruct((spectra.shape[0], far, 2, share, BINS), jnp.bfloat16),
        compiler_params=pltpu.CompilerParams(vmem_limit_bytes=8 * 2**20),
        name="cross",
    )(spectra)


def cross_narrow(spectra, windows, far, share):
    parts, near, rows, width = spectra.shape
    noted = spectra[:, 0, rows - NOTE : rows - NOTE + 2, 0].astype(jnp.int32)
    parted = spectra[:, :, : rows - NOTE].reshape(parts, near, far, windows, 2, share, width)
    first = parted[noted[:, 0]].astype(jnp.float32)
    second = parted[noted[:, 1]].astype(jnp.float32)
    first_re, first_im, second_re, second_im = first[..., 0, :, :], first[..., 1, :, :], second[..., 0, :, :], second[..., 1, :, :]
    real = jnp.sum(first_re * second_re + first_im * second_im, axis=(1, 3))
    imag = jnp.sum(first_re * second_im - first_im * second_re, axis=(1, 3))
    return jnp.stack((real, imag), axis=2)[:, ::-1].astype(jnp.bfloat16)


def inverse_kernel(cross_ref, table_ref, out_ref):
    depth = NB
    far, share = cross_ref.shape[2], cross_ref.shape[4]

    def lags(parity):
        groups = range(parity * GROUPS // PARITIES, (parity + 1) * GROUPS // PARITIES)
        parts = [
            jnp.concatenate([cross_ref[g, h, f, part] for g in groups for part in range(2)], axis=1)
            for f in range(far)
            for h in range(SPLIT)
        ]
        table = table_ref[parity * depth : (parity + 1) * depth]
        product = jnp.dot(jnp.concatenate(parts, axis=0), table, preferred_element_type=jnp.float32)
        return sum(product[f * SPLIT * share : (f + 1) * SPLIT * share] for f in range(far))

    a, b = lags(0), lags(1)
    out_ref[0, :, : LAGS // 2] = a + b
    out_ref[0, :, LAGS // 2 :] = a - b


def inverse(cross, scale):
    vmem = pl.BlockSpec(memory_space=pltpu.VMEM)
    return pl.pallas_call(
        inverse_kernel,
        in_specs=[vmem, vmem],
        out_specs=vmem,
        out_shape=jax.ShapeDtypeStruct((1, SPLIT * cross.shape[4], LAGS), jnp.float32),
        compiler_params=pltpu.CompilerParams(vmem_limit_bytes=16 * 2**20),
        name="inverse",
    )(cross, jnp.asarray(inverse_table(scale)))


def exchange_order(parts):
    return [i ^ (parts // 2 + 1) for i in range(parts)]


def all_to_all(sent, order, axis):
    size = lax.axis_size(axis)
    group = [i * size + size - 1 - k for i in order for k in range(size)]
    return lax.all_to_all(
        sent, ("pair", axis), split_axis=0, concat_axis=0, tiled=True, axis_index_groups=[group]
    )


def local(traces, pairs, block_row):
    _, channels, samples = traces.shape
    windows = samples // WIN
    parts, far, near = lax.axis_size("pair"), lax.axis_size("far"), lax.axis_size("near")
    per_group = parts // (GROUPS * SPLIT)
    share = channels // (far * near * SPLIT)
    width = BINS // per_group
    rows = 2 * far * windows * share + NOTE
    sent = whiten(pairs, block_row, traces[0], windows, far, near)
    if per_group > 1:
        sent = sent.reshape(GROUPS, SPLIT, near, rows, per_group, width).transpose(0, 4, 1, 2, 3, 5)
    order = exchange_order(parts)
    held = all_to_all(sent.reshape(parts * near, rows, width), order, "near")
    cross_of = cross_groups if per_group == 1 else cross_narrow
    cross = cross_of(held.reshape(parts, near, rows, width), windows, far, share)
    mine = all_to_all(cross.reshape(parts * far, 2, share, width), order, "far")
    mine = mine.reshape(GROUPS, per_group, SPLIT, far, 2, share, width)
    mine = mine.transpose(0, 2, 3, 4, 5, 1, 6).reshape(GROUPS, SPLIT, far, 2, share, BINS)
    return inverse(mine, 1.0 / (windows * far * near))


def solution(mesh):
    pairs, segs = mesh.devices.shape
    split = jax.sharding.Mesh(mesh.devices.reshape(pairs, segs // NEAR, NEAR), ("pair", "far", "near"))
    placed = (P("pair", None, ("far", "near")), P("pair", None), P())
    return jax.shard_map(
        local, mesh=split, in_specs=placed, out_specs=P("pair", ("far", "near"), None), check_vma=False
    )
```

```python
import functools

import jax
import jax.numpy as jnp
import ml_dtypes
import numpy as np
from jax import lax
from jax.experimental import pallas as pl
from jax.experimental.pallas import tpu as pltpu
from jax.sharding import PartitionSpec as P

WIN = 2048
NB = 512
LAGS = 2048
HALF = WIN // 2
BINS = 128
GROUPS = NB // BINS
SPLIT = 2
PARITIES = 2
NOTE = 8
OUTER = 2


def frequencies():
    even = np.arange(2, NB + 1, 2)
    odd = np.arange(1, NB + 1, 2)
    return np.concatenate((even, odd)).reshape(GROUPS, BINS)


def forward_table():
    phase = (frequencies()[:, :, None] * np.arange(HALF) % WIN) * (2.0 * np.pi / WIN)
    table = np.stack((np.cos(phase), -np.sin(phase)), axis=1).reshape(PARITIES, NB, HALF)
    return np.ascontiguousarray(table.transpose(0, 2, 1)).astype(ml_dtypes.bfloat16)


def inverse_table(scale):
    shifts = np.arange(LAGS // 2) - LAGS // 2
    phase = (frequencies()[:, :, None] * shifts % WIN) * (2.0 * np.pi / WIN)
    table = np.stack((np.cos(phase), -np.sin(phase)), axis=1) * scale
    return table.reshape(2 * NB, LAGS // 2).astype(ml_dtypes.bfloat16)


def whiten_kernel(windows, inner, outer, pairs_hbm, row_hbm, traces_hbm, table_hbm, sent, pairs_ref, row_ref, frames, table, small_sem, frame_sem, table_sem):
    channels = frames.shape[1]
    share = channels // (inner * outer * SPLIT)
    loads = [
        pltpu.make_async_copy(traces_hbm.at[:, pl.ds(w * WIN, WIN)], frames.at[w], frame_sem.at[w])
        for w in range(windows)
    ]
    tables = [
        pltpu.make_async_copy(table_hbm.at[i], table.at[i], table_sem.at[i]) for i in range(PARITIES)
    ]
    small = [
        pltpu.make_async_copy(source, target, small_sem.at[k])
        for k, (source, target) in enumerate(((pairs_hbm, pairs_ref), (row_hbm, row_ref)))
    ]
    per = GROUPS // PARITIES
    tables[0].start()
    for load in loads:
        load.start()
    tables[1].start()
    for load in small:
        load.start()

    def one(w, i):
        halves = jnp.concatenate((frames[w, :, :HALF], frames[w, :, HALF:]), axis=0)
        product = jnp.dot(halves, table[i], preferred_element_type=jnp.float32)
        first, second = product[:channels], product[channels:]
        spectra = first + second if i == 0 else first - second
        for k in range(per):
            real = spectra[:, 2 * k * BINS : (2 * k + 1) * BINS]
            imag = spectra[:, (2 * k + 1) * BINS : (2 * k + 2) * BINS]
            power = jnp.sum(real * real + imag * imag, axis=0, keepdims=True) * (1.0 / channels)
            gain = lax.rsqrt(power + 1e-06)
            for part, values in enumerate((real, imag)):
                white = (values * gain).astype(jnp.bfloat16).reshape(outer, inner, SPLIT, share, BINS)
                for f in range(inner):
                    at = (2 * (f * windows + w) + part) * share
                    for h in range(SPLIT):
                        for n in range(outer):
                            sent[i * per + k, h, outer - 1 - n, at : at + share] = white[n, f, h]

    early = windows // 2
    tables[0].wait()
    for w in range(early):
        loads[w].wait()
    for w in range(early):
        one(w, 0)
    for w in range(early, windows):
        loads[w].wait()
    tables[1].wait()
    for load in small:
        load.wait()
    turn = row_ref.shape[0] // 2 + 1
    first_row = (row_ref[pairs_ref[0, 0]] ^ turn).astype(jnp.float32)
    second_row = (row_ref[pairs_ref[0, 1]] ^ turn).astype(jnp.float32)
    line = lax.broadcasted_iota(jnp.int32, (NOTE, BINS), 0)
    note = jnp.where(line == 0, first_row, second_row).astype(jnp.bfloat16)
    sent[:, :, :, 2 * inner * windows * share :] = jnp.broadcast_to(note, (GROUPS, SPLIT, outer, NOTE, BINS))
    for w in range(early, windows):
        one(w, 0)
    for w in range(windows):
        one(w, 1)


def in_hbm(values):
    return pltpu.with_memory_space_constraint(values, pltpu.HBM)


def whiten(pairs, block_row, traces, windows, inner, outer):
    channels = traces.shape[0]
    share = channels // (inner * outer * SPLIT)
    shape = (GROUPS, SPLIT, outer, 2 * inner * windows * share + NOTE, BINS)
    hbm = pl.BlockSpec(memory_space=pl.ANY)
    return pl.pallas_call(
        functools.partial(whiten_kernel, windows, inner, outer),
        in_specs=[hbm, hbm, hbm, hbm],
        out_specs=pl.BlockSpec(memory_space=pltpu.VMEM),
        out_shape=pltpu.VMEM(shape, jnp.bfloat16),
        scratch_shapes=[
            pltpu.SMEM(pairs.shape, jnp.int32),
            pltpu.SMEM(block_row.shape, jnp.int32),
            pltpu.VMEM((windows, channels, WIN), jnp.bfloat16),
            pltpu.VMEM((PARITIES, HALF, NB), jnp.bfloat16),
            pltpu.SemaphoreType.DMA((2,)),
            pltpu.SemaphoreType.DMA((windows,)),
            pltpu.SemaphoreType.DMA((PARITIES,)),
        ],
        compiler_params=pltpu.CompilerParams(vmem_limit_bytes=24 * 2**20),
        name="whiten",
    )(*(in_hbm(values) for values in (pairs, block_row, traces, jnp.asarray(forward_table()))))


def cross_kernel(windows, spectra_ref, out_ref):
    count, inner, _, share, _ = out_ref.shape
    outer = spectra_ref.shape[1]
    notes = [spectra_ref[i, 0, 2 * inner * windows * share :].astype(jnp.float32) for i in range(count)]
    rows = [(note[0, 0].astype(jnp.int32), note[1, 0].astype(jnp.int32)) for note in notes]
    for i, (a, b) in enumerate(rows):
        for f in range(inner):
            real = jnp.zeros(out_ref.shape[3:], jnp.float32)
            imag = jnp.zeros(out_ref.shape[3:], jnp.float32)
            for n in range(outer):
                for w in range(windows):
                    at = 2 * (f * windows + w) * share
                    re, im = slice(at, at + share), slice(at + share, at + 2 * share)
                    first_re = spectra_ref[a, n, re].astype(jnp.float32)
                    first_im = spectra_ref[a, n, im].astype(jnp.float32)
                    second_re = spectra_ref[b, n, re].astype(jnp.float32)
                    second_im = spectra_ref[b, n, im].astype(jnp.float32)
                    real += first_re * second_re + first_im * second_im
                    imag += first_re * second_im - first_im * second_re
            out_ref[i, inner - 1 - f, 0] = real.astype(jnp.bfloat16)
            out_ref[i, inner - 1 - f, 1] = imag.astype(jnp.bfloat16)


def cross_groups(spectra, windows, inner, share):
    vmem = pl.BlockSpec(memory_space=pltpu.VMEM)
    return pl.pallas_call(
        functools.partial(cross_kernel, windows),
        in_specs=[vmem],
        out_specs=vmem,
        out_shape=jax.ShapeDtypeStruct((spectra.shape[0], inner, 2, share, BINS), jnp.bfloat16),
        compiler_params=pltpu.CompilerParams(vmem_limit_bytes=8 * 2**20),
        name="cross",
    )(spectra)


def cross_narrow(spectra, windows, inner, share):
    parts, outer, rows, width = spectra.shape
    noted = spectra[:, 0, rows - NOTE : rows - NOTE + 2, 0].astype(jnp.int32)
    parted = spectra[:, :, : rows - NOTE].reshape(parts, outer, inner, windows, 2, share, width)
    first = parted[noted[:, 0]].astype(jnp.float32)
    second = parted[noted[:, 1]].astype(jnp.float32)
    first_re, first_im, second_re, second_im = first[..., 0, :, :], first[..., 1, :, :], second[..., 0, :, :], second[..., 1, :, :]
    real = jnp.sum(first_re * second_re + first_im * second_im, axis=(1, 3))
    imag = jnp.sum(first_re * second_im - first_im * second_re, axis=(1, 3))
    return jnp.stack((real, imag), axis=2)[:, ::-1].astype(jnp.bfloat16)


def inverse_kernel(cross_ref, table_ref, out_ref):
    depth = NB
    inner, share = cross_ref.shape[2], cross_ref.shape[4]

    def lags(parity):
        groups = range(parity * GROUPS // PARITIES, (parity + 1) * GROUPS // PARITIES)
        parts = [
            jnp.concatenate([cross_ref[g, h, f, part] for g in groups for part in range(2)], axis=1)
            for f in range(inner)
            for h in range(SPLIT)
        ]
        table = table_ref[parity * depth : (parity + 1) * depth]
        product = jnp.dot(jnp.concatenate(parts, axis=0), table, preferred_element_type=jnp.float32)
        return sum(product[f * SPLIT * share : (f + 1) * SPLIT * share] for f in range(inner))

    a, b = lags(0), lags(1)
    out_ref[0, :, : LAGS // 2] = a + b
    out_ref[0, :, LAGS // 2 :] = a - b


def inverse(cross, scale):
    vmem = pl.BlockSpec(memory_space=pltpu.VMEM)
    return pl.pallas_call(
        inverse_kernel,
        in_specs=[vmem, vmem],
        out_specs=vmem,
        out_shape=jax.ShapeDtypeStruct((1, SPLIT * cross.shape[4], LAGS), jnp.float32),
        compiler_params=pltpu.CompilerParams(vmem_limit_bytes=16 * 2**20),
        name="inverse",
    )(cross, jnp.asarray(inverse_table(scale)))


def exchange_order(parts):
    return [i ^ (parts // 2 + 1) for i in range(parts)]


def all_to_all(sent, order, axis):
    size = lax.axis_size(axis)
    group = [i * size + size - 1 - k for i in order for k in range(size)]
    return lax.all_to_all(
        sent, ("pair", axis), split_axis=0, concat_axis=0, tiled=True, axis_index_groups=[group]
    )


def local(traces, pairs, block_row):
    _, channels, samples = traces.shape
    windows = samples // WIN
    parts, inner, outer = lax.axis_size("pair"), lax.axis_size("inner"), lax.axis_size("outer")
    per_group = parts // (GROUPS * SPLIT)
    share = channels // (inner * outer * SPLIT)
    width = BINS // per_group
    rows = 2 * inner * windows * share + NOTE
    sent = whiten(pairs, block_row, traces[0], windows, inner, outer)
    if per_group > 1:
        sent = sent.reshape(GROUPS, SPLIT, outer, rows, per_group, width).transpose(0, 4, 1, 2, 3, 5)
    order = exchange_order(parts)
    held = all_to_all(sent.reshape(parts * outer, rows, width), order, "outer")
    cross_of = cross_groups if per_group == 1 else cross_narrow
    cross = cross_of(held.reshape(parts, outer, rows, width), windows, inner, share)
    mine = all_to_all(cross.reshape(parts * inner, 2, share, width), order, "inner")
    mine = mine.reshape(GROUPS, per_group, SPLIT, inner, 2, share, width)
    mine = mine.transpose(0, 2, 3, 4, 5, 1, 6).reshape(GROUPS, SPLIT, inner, 2, share, BINS)
    return inverse(mine, 1.0 / (windows * inner * outer))


def solution(mesh):
    pairs, segs = mesh.devices.shape
    split = jax.sharding.Mesh(mesh.devices.reshape(pairs, OUTER, segs // OUTER), ("pair", "outer", "inner"))
    placed = (P("pair", None, ("outer", "inner")), P("pair", None), P())
    return jax.shard_map(
        local, mesh=split, in_specs=placed, out_specs=P("pair", ("outer", "inner"), None), check_vma=False
    )
```

```python
import functools

import jax
import jax.numpy as jnp
import ml_dtypes
import numpy as np
from jax import lax
from jax.experimental import pallas as pl
from jax.experimental.pallas import tpu as pltpu
from jax.sharding import PartitionSpec as P

WIN = 2048
NB = 512
LAGS = 2048
HALF = WIN // 2
BINS = 128
GROUPS = NB // BINS
SPLIT = 2
PARITIES = 2
NOTE = 16
OUTER = 2


def frequencies():
    even = np.arange(2, NB + 1, 2)
    odd = np.arange(1, NB + 1, 2)
    return np.concatenate((even, odd)).reshape(GROUPS, BINS)


def forward_table():
    phase = (frequencies()[:, :, None] * np.arange(HALF) % WIN) * (2.0 * np.pi / WIN)
    table = np.stack((np.cos(phase), -np.sin(phase)), axis=1).reshape(PARITIES, NB, HALF)
    return np.ascontiguousarray(table.transpose(0, 2, 1)).astype(ml_dtypes.bfloat16)


def inverse_table(scale):
    shifts = np.arange(LAGS // 2) - LAGS // 2
    phase = (frequencies()[:, :, None] * shifts % WIN) * (2.0 * np.pi / WIN)
    table = np.stack((np.cos(phase), -np.sin(phase)), axis=1) * scale
    return table.reshape(2 * NB, LAGS // 2).astype(ml_dtypes.bfloat16)


def whiten_kernel(windows, inner, outer, pairs_hbm, row_hbm, traces_hbm, table_hbm, sent, pairs_ref, row_ref, frames, table, small_sem, frame_sem, table_sem):
    channels = frames.shape[1]
    share = channels // (inner * outer * SPLIT)
    loads = [
        pltpu.make_async_copy(traces_hbm.at[:, pl.ds(w * WIN, WIN)], frames.at[w], frame_sem.at[w])
        for w in range(windows)
    ]
    tables = [
        pltpu.make_async_copy(table_hbm.at[i], table.at[i], table_sem.at[i]) for i in range(PARITIES)
    ]
    small = [
        pltpu.make_async_copy(source, target, small_sem.at[k])
        for k, (source, target) in enumerate(((pairs_hbm, pairs_ref), (row_hbm, row_ref)))
    ]
    per = GROUPS // PARITIES
    tables[0].start()
    for load in loads:
        load.start()
    tables[1].start()
    for load in small:
        load.start()

    def one(w, i):
        halves = jnp.concatenate((frames[w, :, :HALF], frames[w, :, HALF:]), axis=0)
        product = jnp.dot(halves, table[i], preferred_element_type=jnp.float32)
        first, second = product[:channels], product[channels:]
        spectra = first + second if i == 0 else first - second
        for k in range(per):
            real = spectra[:, 2 * k * BINS : (2 * k + 1) * BINS]
            imag = spectra[:, (2 * k + 1) * BINS : (2 * k + 2) * BINS]
            power = jnp.sum(real * real + imag * imag, axis=0, keepdims=True) * (1.0 / channels)
            gain = lax.rsqrt(power + 1e-06)
            for part, values in enumerate((real, imag)):
                white = (values * gain).astype(jnp.bfloat16).reshape(outer, inner, SPLIT, share, BINS)
                for f in range(inner):
                    at = (2 * (f * windows + w) + part) * share
                    for h in range(SPLIT):
                        for n in range(outer):
                            sent[i * per + k, h, outer - 1 - n, at : at + share] = white[n, f, h]

    early = windows // 2
    tables[0].wait()
    for w in range(early):
        loads[w].wait()
    for w in range(early):
        one(w, 0)
    for w in range(early, windows):
        loads[w].wait()
    tables[1].wait()
    for load in small:
        load.wait()
    turn = row_ref.shape[0] // 2 + 1
    first_row = (row_ref[pairs_ref[0, 0]] ^ turn).astype(jnp.float32)
    second_row = (row_ref[pairs_ref[0, 1]] ^ turn).astype(jnp.float32)
    line = lax.broadcasted_iota(jnp.int32, (NOTE, BINS), 0)
    note = jnp.where(line == 0, first_row, second_row).astype(jnp.bfloat16)
    sent[:, :, :, 2 * inner * windows * share :] = jnp.broadcast_to(note, (GROUPS, SPLIT, outer, NOTE, BINS))
    for w in range(early, windows):
        one(w, 0)
    for w in range(windows):
        one(w, 1)


def in_hbm(values):
    return pltpu.with_memory_space_constraint(values, pltpu.HBM)


def whiten(pairs, block_row, traces, windows, inner, outer):
    channels = traces.shape[0]
    share = channels // (inner * outer * SPLIT)
    shape = (GROUPS, SPLIT, outer, 2 * inner * windows * share + NOTE, BINS)
    hbm = pl.BlockSpec(memory_space=pl.ANY)
    return pl.pallas_call(
        functools.partial(whiten_kernel, windows, inner, outer),
        in_specs=[hbm, hbm, hbm, hbm],
        out_specs=pl.BlockSpec(memory_space=pltpu.VMEM),
        out_shape=pltpu.VMEM(shape, jnp.bfloat16),
        scratch_shapes=[
            pltpu.SMEM(pairs.shape, jnp.int32),
            pltpu.SMEM(block_row.shape, jnp.int32),
            pltpu.VMEM((windows, channels, WIN), jnp.bfloat16),
            pltpu.VMEM((PARITIES, HALF, NB), jnp.bfloat16),
            pltpu.SemaphoreType.DMA((2,)),
            pltpu.SemaphoreType.DMA((windows,)),
            pltpu.SemaphoreType.DMA((PARITIES,)),
        ],
        compiler_params=pltpu.CompilerParams(vmem_limit_bytes=24 * 2**20),
        name="whiten",
    )(*(in_hbm(values) for values in (pairs, block_row, traces, jnp.asarray(forward_table()))))


def cross_kernel(windows, spectra_ref, out_ref):
    count, inner, _, share, _ = out_ref.shape
    outer = spectra_ref.shape[1]
    notes = [spectra_ref[i, 0, 2 * inner * windows * share :].astype(jnp.float32) for i in range(count)]
    rows = [(note[0, 0].astype(jnp.int32), note[1, 0].astype(jnp.int32)) for note in notes]
    for i, (a, b) in enumerate(rows):
        for f in range(inner):
            real = jnp.zeros(out_ref.shape[3:], jnp.float32)
            imag = jnp.zeros(out_ref.shape[3:], jnp.float32)
            for n in range(outer):
                for w in range(windows):
                    at = 2 * (f * windows + w) * share
                    re, im = slice(at, at + share), slice(at + share, at + 2 * share)
                    first_re = spectra_ref[a, n, re].astype(jnp.float32)
                    first_im = spectra_ref[a, n, im].astype(jnp.float32)
                    second_re = spectra_ref[b, n, re].astype(jnp.float32)
                    second_im = spectra_ref[b, n, im].astype(jnp.float32)
                    real += first_re * second_re + first_im * second_im
                    imag += first_re * second_im - first_im * second_re
            out_ref[i, inner - 1 - f, 0] = real.astype(jnp.bfloat16)
            out_ref[i, inner - 1 - f, 1] = imag.astype(jnp.bfloat16)


def cross_groups(spectra, windows, inner, share):
    vmem = pl.BlockSpec(memory_space=pltpu.VMEM)
    return pl.pallas_call(
        functools.partial(cross_kernel, windows),
        in_specs=[vmem],
        out_specs=vmem,
        out_shape=jax.ShapeDtypeStruct((spectra.shape[0], inner, 2, share, BINS), jnp.bfloat16),
        compiler_params=pltpu.CompilerParams(vmem_limit_bytes=8 * 2**20),
        name="cross",
    )(spectra)


def cross_narrow(spectra, windows, inner, share):
    parts, outer, rows, width = spectra.shape
    noted = spectra[:, 0, rows - NOTE : rows - NOTE + 2, 0].astype(jnp.int32)
    parted = spectra[:, :, : rows - NOTE].reshape(parts, outer, inner, windows, 2, share, width)
    first = parted[noted[:, 0]].astype(jnp.float32)
    second = parted[noted[:, 1]].astype(jnp.float32)
    first_re, first_im, second_re, second_im = first[..., 0, :, :], first[..., 1, :, :], second[..., 0, :, :], second[..., 1, :, :]
    real = jnp.sum(first_re * second_re + first_im * second_im, axis=(1, 3))
    imag = jnp.sum(first_re * second_im - first_im * second_re, axis=(1, 3))
    return jnp.stack((real, imag), axis=2)[:, ::-1].astype(jnp.bfloat16)


def inverse_kernel(cross_ref, table_ref, out_ref):
    depth = NB
    inner, share = cross_ref.shape[2], cross_ref.shape[4]

    def lags(parity):
        groups = range(parity * GROUPS // PARITIES, (parity + 1) * GROUPS // PARITIES)
        parts = [
            jnp.concatenate([cross_ref[g, h, f, part] for g in groups for part in range(2)], axis=1)
            for f in range(inner)
            for h in range(SPLIT)
        ]
        table = table_ref[parity * depth : (parity + 1) * depth]
        product = jnp.dot(jnp.concatenate(parts, axis=0), table, preferred_element_type=jnp.float32)
        return sum(product[f * SPLIT * share : (f + 1) * SPLIT * share] for f in range(inner))

    a, b = lags(0), lags(1)
    out_ref[0, :, : LAGS // 2] = a + b
    out_ref[0, :, LAGS // 2 :] = a - b


def inverse(cross, scale):
    vmem = pl.BlockSpec(memory_space=pltpu.VMEM)
    return pl.pallas_call(
        inverse_kernel,
        in_specs=[vmem, vmem],
        out_specs=vmem,
        out_shape=jax.ShapeDtypeStruct((1, SPLIT * cross.shape[4], LAGS), jnp.float32),
        compiler_params=pltpu.CompilerParams(vmem_limit_bytes=16 * 2**20),
        name="inverse",
    )(cross, jnp.asarray(inverse_table(scale)))


def exchange_order(parts):
    return [i ^ (parts // 2 + 1) for i in range(parts)]


def all_to_all(sent, order, axis):
    size = lax.axis_size(axis)
    group = [i * size + size - 1 - k for i in order for k in range(size)]
    return lax.all_to_all(
        sent, ("pair", axis), split_axis=0, concat_axis=0, tiled=True, axis_index_groups=[group]
    )


def local(traces, pairs, block_row):
    _, channels, samples = traces.shape
    windows = samples // WIN
    parts, inner, outer = lax.axis_size("pair"), lax.axis_size("inner"), lax.axis_size("outer")
    per_group = parts // (GROUPS * SPLIT)
    share = channels // (inner * outer * SPLIT)
    width = BINS // per_group
    rows = 2 * inner * windows * share + NOTE
    sent = whiten(pairs, block_row, traces[0], windows, inner, outer)
    if per_group > 1:
        sent = sent.reshape(GROUPS, SPLIT, outer, rows, per_group, width).transpose(0, 4, 1, 2, 3, 5)
    order = exchange_order(parts)
    held = all_to_all(sent.reshape(parts * outer, rows, width), order, "outer")
    cross_of = cross_groups if per_group == 1 else cross_narrow
    cross = cross_of(held.reshape(parts, outer, rows, width), windows, inner, share)
    mine = all_to_all(cross.reshape(parts * inner, 2, share, width), order, "inner")
    mine = mine.reshape(GROUPS, per_group, SPLIT, inner, 2, share, width)
    mine = mine.transpose(0, 2, 3, 4, 5, 1, 6).reshape(GROUPS, SPLIT, inner, 2, share, BINS)
    return inverse(mine, 1.0 / (windows * inner * outer))


def solution(mesh):
    pairs, segs = mesh.devices.shape
    split = jax.sharding.Mesh(mesh.devices.reshape(pairs, OUTER, segs // OUTER), ("pair", "outer", "inner"))
    placed = (P("pair", None, ("outer", "inner")), P("pair", None), P())
    return jax.shard_map(
        local, mesh=split, in_specs=placed, out_specs=P("pair", ("outer", "inner"), None), check_vma=False
    )
```

```python
import functools

import jax
import jax.numpy as jnp
import ml_dtypes
import numpy as np
from jax import lax
from jax.experimental import pallas as pl
from jax.experimental.pallas import tpu as pltpu
from jax.sharding import PartitionSpec as P

WIN = 2048
NB = 512
LAGS = 2048
HALF = WIN // 2
BINS = 128
GROUPS = NB // BINS
SPLIT = 2
PARITIES = 2
NOTE = 8
OUTER = 2


def frequencies():
    return np.stack([np.arange(first, NB + 1, 4) for first in (4, 2, 1, 3)])


def forward_table():
    phase = (frequencies()[:, :, None] * np.arange(HALF) % WIN) * (2.0 * np.pi / WIN)
    table = np.stack((np.cos(phase), -np.sin(phase)), axis=1).reshape(PARITIES, NB, HALF)
    return np.ascontiguousarray(table.transpose(0, 2, 1)).astype(ml_dtypes.bfloat16)


def inverse_table(scale):
    shifts = np.arange(LAGS // 4) - LAGS // 2
    phase = (frequencies()[:, :, None] * shifts % WIN) * (2.0 * np.pi / WIN)
    table = np.stack((np.cos(phase), -np.sin(phase)), axis=1) * scale
    return table.reshape(2 * NB, LAGS // 4).astype(ml_dtypes.bfloat16)


def whiten_kernel(windows, inner, outer, pairs_hbm, row_hbm, traces_hbm, table_hbm, sent, pairs_ref, row_ref, frames, table, small_sem, frame_sem, table_sem):
    channels = frames.shape[1]
    share = channels // (inner * outer * SPLIT)
    loads = [
        pltpu.make_async_copy(traces_hbm.at[:, pl.ds(w * WIN, WIN)], frames.at[w], frame_sem.at[w])
        for w in range(windows)
    ]
    tables = [
        pltpu.make_async_copy(table_hbm.at[i], table.at[i], table_sem.at[i]) for i in range(PARITIES)
    ]
    small = [
        pltpu.make_async_copy(source, target, small_sem.at[k])
        for k, (source, target) in enumerate(((pairs_hbm, pairs_ref), (row_hbm, row_ref)))
    ]
    per = GROUPS // PARITIES
    tables[0].start()
    for load in loads:
        load.start()
    tables[1].start()
    for load in small:
        load.start()

    def one(w, i):
        halves = jnp.concatenate((frames[w, :, :HALF], frames[w, :, HALF:]), axis=0)
        product = jnp.dot(halves, table[i], preferred_element_type=jnp.float32)
        first, second = product[:channels], product[channels:]
        spectra = first + second if i == 0 else first - second
        for k in range(per):
            real = spectra[:, 2 * k * BINS : (2 * k + 1) * BINS]
            imag = spectra[:, (2 * k + 1) * BINS : (2 * k + 2) * BINS]
            power = jnp.sum(real * real + imag * imag, axis=0, keepdims=True) * (1.0 / channels)
            gain = lax.rsqrt(power + 1e-06)
            for part, values in enumerate((real, imag)):
                white = (values * gain).astype(jnp.bfloat16).reshape(outer, inner, SPLIT, share, BINS)
                for f in range(inner):
                    at = (2 * (f * windows + w) + part) * share
                    for h in range(SPLIT):
                        for n in range(outer):
                            sent[i * per + k, h, outer - 1 - n, at : at + share] = white[n, f, h]

    early = windows // 2
    tables[0].wait()
    for w in range(early):
        loads[w].wait()
    for w in range(early):
        one(w, 0)
    for w in range(early, windows):
        loads[w].wait()
    tables[1].wait()
    for load in small:
        load.wait()
    turn = row_ref.shape[0] // 2 + 1
    first_row = (row_ref[pairs_ref[0, 0]] ^ turn).astype(jnp.float32)
    second_row = (row_ref[pairs_ref[0, 1]] ^ turn).astype(jnp.float32)
    line = lax.broadcasted_iota(jnp.int32, (NOTE, BINS), 0)
    note = jnp.where(line == 0, first_row, second_row).astype(jnp.bfloat16)
    sent[:, :, :, 2 * inner * windows * share :] = jnp.broadcast_to(note, (GROUPS, SPLIT, outer, NOTE, BINS))
    for w in range(early, windows):
        one(w, 0)
    for w in range(windows):
        one(w, 1)


def in_hbm(values):
    return pltpu.with_memory_space_constraint(values, pltpu.HBM)


def whiten(pairs, block_row, traces, windows, inner, outer):
    channels = traces.shape[0]
    share = channels // (inner * outer * SPLIT)
    shape = (GROUPS, SPLIT, outer, 2 * inner * windows * share + NOTE, BINS)
    hbm = pl.BlockSpec(memory_space=pl.ANY)
    return pl.pallas_call(
        functools.partial(whiten_kernel, windows, inner, outer),
        in_specs=[hbm, hbm, hbm, hbm],
        out_specs=pl.BlockSpec(memory_space=pltpu.VMEM),
        out_shape=pltpu.VMEM(shape, jnp.bfloat16),
        scratch_shapes=[
            pltpu.SMEM(pairs.shape, jnp.int32),
            pltpu.SMEM(block_row.shape, jnp.int32),
            pltpu.VMEM((windows, channels, WIN), jnp.bfloat16),
            pltpu.VMEM((PARITIES, HALF, NB), jnp.bfloat16),
            pltpu.SemaphoreType.DMA((2,)),
            pltpu.SemaphoreType.DMA((windows,)),
            pltpu.SemaphoreType.DMA((PARITIES,)),
        ],
        compiler_params=pltpu.CompilerParams(vmem_limit_bytes=24 * 2**20),
        name="whiten",
    )(*(in_hbm(values) for values in (pairs, block_row, traces, jnp.asarray(forward_table()))))


def cross_kernel(windows, spectra_ref, out_ref):
    count, inner, _, share, _ = out_ref.shape
    outer = spectra_ref.shape[1]
    notes = [spectra_ref[i, 0, 2 * inner * windows * share :].astype(jnp.float32) for i in range(count)]
    rows = [(note[0, 0].astype(jnp.int32), note[1, 0].astype(jnp.int32)) for note in notes]
    for i, (a, b) in enumerate(rows):
        for f in range(inner):
            real = jnp.zeros(out_ref.shape[3:], jnp.float32)
            imag = jnp.zeros(out_ref.shape[3:], jnp.float32)
            for n in range(outer):
                for w in range(windows):
                    at = 2 * (f * windows + w) * share
                    re, im = slice(at, at + share), slice(at + share, at + 2 * share)
                    first_re = spectra_ref[a, n, re].astype(jnp.float32)
                    first_im = spectra_ref[a, n, im].astype(jnp.float32)
                    second_re = spectra_ref[b, n, re].astype(jnp.float32)
                    second_im = spectra_ref[b, n, im].astype(jnp.float32)
                    real += first_re * second_re + first_im * second_im
                    imag += first_re * second_im - first_im * second_re
            out_ref[i, inner - 1 - f, 0] = real.astype(jnp.bfloat16)
            out_ref[i, inner - 1 - f, 1] = imag.astype(jnp.bfloat16)


def cross_groups(spectra, windows, inner, share):
    vmem = pl.BlockSpec(memory_space=pltpu.VMEM)
    return pl.pallas_call(
        functools.partial(cross_kernel, windows),
        in_specs=[vmem],
        out_specs=vmem,
        out_shape=jax.ShapeDtypeStruct((spectra.shape[0], inner, 2, share, BINS), jnp.bfloat16),
        compiler_params=pltpu.CompilerParams(vmem_limit_bytes=8 * 2**20),
        name="cross",
    )(spectra)


def cross_narrow(spectra, windows, inner, share):
    parts, outer, rows, width = spectra.shape
    noted = spectra[:, 0, rows - NOTE : rows - NOTE + 2, 0].astype(jnp.int32)
    parted = spectra[:, :, : rows - NOTE].reshape(parts, outer, inner, windows, 2, share, width)
    first = parted[noted[:, 0]].astype(jnp.float32)
    second = parted[noted[:, 1]].astype(jnp.float32)
    first_re, first_im, second_re, second_im = first[..., 0, :, :], first[..., 1, :, :], second[..., 0, :, :], second[..., 1, :, :]
    real = jnp.sum(first_re * second_re + first_im * second_im, axis=(1, 3))
    imag = jnp.sum(first_re * second_im - first_im * second_re, axis=(1, 3))
    return jnp.stack((real, imag), axis=2)[:, ::-1].astype(jnp.bfloat16)


def inverse_kernel(cross_ref, table_ref, out_ref):
    inner, share = cross_ref.shape[2], cross_ref.shape[4]
    rows, quarter = SPLIT * share, LAGS // 4

    def lags(parity):
        parts = []
        for turned in range(2):
            for f in range(inner):
                for h in range(SPLIT):
                    (re0, im0), (re1, im1) = (
                        (cross_ref[g, h, f, 0], cross_ref[g, h, f, 1]) for g in (2 * parity, 2 * parity + 1)
                    )
                    if turned and parity == 0:
                        re1, im1 = -re1, -im1
                    elif turned:
                        re0, im0, re1, im1 = -im0, re0, im1, -re1
                    parts.append(jnp.concatenate((re0, im0, re1, im1), axis=1))
        table = table_ref[parity * NB : (parity + 1) * NB]
        product = jnp.dot(jnp.concatenate(parts, axis=0), table, preferred_element_type=jnp.float32)
        return [
            sum(product[(q * inner + f) * rows : (q * inner + f + 1) * rows] for f in range(inner)) for q in range(2)
        ]

    even, odd = lags(0), lags(1)
    for q in range(4):
        a, b = even[q % 2], odd[q % 2]
        out_ref[0, :, q * quarter : (q + 1) * quarter] = a + b if q < 2 else a - b


def inverse(cross, scale):
    vmem = pl.BlockSpec(memory_space=pltpu.VMEM)
    return pl.pallas_call(
        inverse_kernel,
        in_specs=[vmem, vmem],
        out_specs=vmem,
        out_shape=jax.ShapeDtypeStruct((1, SPLIT * cross.shape[4], LAGS), jnp.float32),
        compiler_params=pltpu.CompilerParams(vmem_limit_bytes=16 * 2**20),
        name="inverse",
    )(cross, jnp.asarray(inverse_table(scale)))


def exchange_order(parts):
    return [i ^ (parts // 2 + 1) for i in range(parts)]


def all_to_all(sent, order, axis):
    size = lax.axis_size(axis)
    group = [i * size + size - 1 - k for i in order for k in range(size)]
    return lax.all_to_all(
        sent, ("pair", axis), split_axis=0, concat_axis=0, tiled=True, axis_index_groups=[group]
    )


def local(traces, pairs, block_row):
    _, channels, samples = traces.shape
    windows = samples // WIN
    parts, inner, outer = lax.axis_size("pair"), lax.axis_size("inner"), lax.axis_size("outer")
    per_group = parts // (GROUPS * SPLIT)
    share = channels // (inner * outer * SPLIT)
    width = BINS // per_group
    rows = 2 * inner * windows * share + NOTE
    sent = whiten(pairs, block_row, traces[0], windows, inner, outer)
    if per_group > 1:
        sent = sent.reshape(GROUPS, SPLIT, outer, rows, per_group, width).transpose(0, 4, 1, 2, 3, 5)
    order = exchange_order(parts)
    held = all_to_all(sent.reshape(parts * outer, rows, width), order, "outer")
    cross_of = cross_groups if per_group == 1 else cross_narrow
    cross = cross_of(held.reshape(parts, outer, rows, width), windows, inner, share)
    mine = all_to_all(cross.reshape(parts * inner, 2, share, width), order, "inner")
    mine = mine.reshape(GROUPS, per_group, SPLIT, inner, 2, share, width)
    mine = mine.transpose(0, 2, 3, 4, 5, 1, 6).reshape(GROUPS, SPLIT, inner, 2, share, BINS)
    return inverse(mine, 1.0 / (windows * inner * outer))


def solution(mesh):
    pairs, segs = mesh.devices.shape
    split = jax.sharding.Mesh(mesh.devices.reshape(pairs, OUTER, segs // OUTER), ("pair", "outer", "inner"))
    placed = (P("pair", None, ("outer", "inner")), P("pair", None), P())
    return jax.shard_map(
        local, mesh=split, in_specs=placed, out_specs=P("pair", ("outer", "inner"), None), check_vma=False
    )
```
